256 devices in a mesh: pencil: 16 (over x, y), band: 16 (over z, core).
Axes of the slice: x: 4, y: 4, z: 8, core: 2. Of those that a mesh axis runs over, the one named last changes fastest.
Arguments:
- coeffs: float32 [16, 512, 224], P('band', 'pencil'), may hold values from -16 to 16
- columns: int32 [512], replicated, may hold values from 0 to 12543, as said below
- potential: float32 [112, 12544], P('pencil'), may hold values from -5 to 5
- ritz_vectors: float32 [2, 16, 16], replicated, may hold values from -1 to 2
Outputs:
- refined_coeffs: float32 [16, 512, 224], P('band', 'pencil')
- refined_hcoeffs: float32 [16, 512, 224], P('band', 'pencil')
- ritz_values: float32 [16], replicated
The draws below stay inside these ranges and needn't reach their ends.
Inputs may be any that keep to these rules, and one draw needn't show every extreme that they name: The 512 entries are distinct columns ix * 112 + iy with f(ix)^2 + f(iy)^2 <= 28^2; stick s belongs to pencil device s // 32.
All inputs are finite; a program needn't handle non-finite values.
Results may differ from the reference program's by a relative error of at most 0.0003.
Values sent between devices are 32-bit elements; how exact they have to be, the bound alone decides.
A program may use at most 64 MiB of HBM per device.

```python
import jax
import jax.numpy as jnp
from jax import lax

GRID = 112
NB = 16
STICKS = 512


def draw_coeffs(key, part):
    radius = GRID // 4
    width_key = jax.random.fold_in(key, 11)
    values_key = jax.random.fold_in(key, 12)
    spread = jax.random.uniform(width_key, (NB,), jnp.float32, jnp.log(0.15), jnp.log(2.5))
    widths = radius * jnp.exp(spread)
    indices = jnp.arange(GRID, dtype=jnp.int32)
    waves = jnp.where(indices < GRID // 2, indices, indices - GRID).astype(jnp.float32)
    envelope = jnp.exp(-0.5 * (waves[None, :] / widths[:, None]) ** 2)
    envelope = envelope / jnp.sqrt(2.0 * jnp.mean(envelope * envelope, axis=1, keepdims=True))
    envelope = jnp.concatenate([envelope, envelope], axis=1)
    fluctuation = jnp.clip(jax.random.normal(values_key, (NB, STICKS, 2 * GRID), jnp.float32), -4.0, 4.0)
    return fluctuation * envelope[:, None, :]


def draw_columns(key, part):
    radius = GRID // 4
    order_key = jax.random.fold_in(key, 21)
    cells = jnp.arange(GRID * GRID, dtype=jnp.int32)
    wave_x = jnp.where(cells // GRID < GRID // 2, cells // GRID, cells // GRID - GRID)
    wave_y = jnp.where(cells % GRID < GRID // 2, cells % GRID, cells % GRID - GRID)
    inside = wave_x * wave_x + wave_y * wave_y <= radius * radius
    ranks = jax.random.permutation(order_key, GRID * GRID).astype(jnp.int32)
    scores = jnp.where(inside, ranks, ranks + GRID * GRID)
    ordering = jnp.argsort(scores, stable=True).astype(jnp.int32)
    return ordering[:STICKS]


def draw_potential(key, part):
    offset_key = jax.random.fold_in(key, 31)
    field_key = jax.random.fold_in(key, 32)
    offset = jax.random.uniform(offset_key, (), jnp.float32, -1.0, 1.0)
    roughness = jnp.clip(jax.random.normal(field_key, (GRID, GRID * GRID), jnp.float32), -4.0, 4.0)
    return offset + roughness


def draw_ritz_vectors(key, part):
    real_key = jax.random.fold_in(key, 41)
    imag_key = jax.random.fold_in(key, 42)
    strength = 0.25 / jnp.sqrt(float(NB))
    real_noise = jnp.clip(jax.random.normal(real_key, (NB, NB), jnp.float32), -4.0, 4.0)
    imag_noise = jnp.clip(jax.random.normal(imag_key, (NB, NB), jnp.float32), -4.0, 4.0)
    identity = jnp.eye(NB, dtype=jnp.float32)
    return jnp.stack([identity + strength * real_noise, strength * imag_noise], axis=0)


def setup_inputs(seed: int = 0) -> dict:
    keys = jax.random.split(jax.random.key(seed), 5)
    return {
        "coeffs": draw_coeffs(jax.random.fold_in(keys[4], 71), 0),
        "columns": draw_columns(jax.random.fold_in(keys[4], 71), 0),
        "potential": draw_potential(jax.random.fold_in(keys[4], 71), 0),
        "ritz_vectors": draw_ritz_vectors(jax.random.fold_in(keys[4], 71), 0),
    }


precise = lax.Precision.HIGHEST


def frequencies(indices, length):
    return jnp.where(indices < length // 2, indices, indices - length)


def kinetic_table(columns, grid_size):
    radius = grid_size // 4
    wave_x = frequencies(columns // grid_size, grid_size).astype(jnp.float32)
    wave_y = frequencies(columns % grid_size, grid_size).astype(jnp.float32)
    wave_z = frequencies(jnp.arange(grid_size, dtype=jnp.int32), grid_size).astype(jnp.float32)
    lateral = wave_x * wave_x + wave_y * wave_y
    return 0.5 * (lateral[:, None] + (wave_z * wave_z)[None, :]) / float(radius * radius)


def swap_halves(values):
    half_width = values.shape[-1] // 2
    return jnp.concatenate([values[..., half_width:], -values[..., :half_width]], axis=-1)


def complex_product(left_real, left_imag, right_real, right_imag):
    out_real = jnp.dot(left_real, right_real, precision=precise) - jnp.dot(left_imag, right_imag, precision=precise)
    out_imag = jnp.dot(left_real, right_imag, precision=precise) + jnp.dot(left_imag, right_real, precision=precise)
    return out_real, out_imag


def refine(over_real, over_imag, ham_real, ham_imag, vector_real, vector_imag):
    band_total = vector_real.shape[0]
    adjoint_real = vector_real.T
    adjoint_imag = -vector_imag.T
    temp_real, temp_imag = complex_product(over_real, over_imag, vector_real, vector_imag)
    metric_real, metric_imag = complex_product(adjoint_real, adjoint_imag, temp_real, temp_imag)
    temp_real, temp_imag = complex_product(ham_real, ham_imag, vector_real, vector_imag)
    energy_real, energy_imag = complex_product(adjoint_real, adjoint_imag, temp_real, temp_imag)
    identity = jnp.eye(band_total, dtype=vector_real.dtype)
    residual_real = identity - metric_real
    residual_imag = -metric_imag
    values = jnp.diagonal(energy_real) / jnp.diagonal(metric_real)
    spacing = values[None, :] - values[:, None]
    floor_value = (0.25 / band_total) ** 2
    factor = spacing / jnp.maximum(spacing * spacing, floor_value)
    upper_real = energy_real + values[None, :] * residual_real
    upper_imag = energy_imag + values[None, :] * residual_imag
    on_diagonal = identity > 0.5
    update_real = jnp.where(on_diagonal, 0.5 * residual_real, upper_real * factor)
    update_imag = jnp.where(on_diagonal, 0.5 * residual_imag, upper_imag * factor)
    change_real, change_imag = complex_product(vector_real, vector_imag, update_real, update_imag)
    return vector_real + change_real, vector_imag + change_imag, values


def rotate(flat_values, turned_values, new_real, new_imag):
    stacked = jnp.concatenate([flat_values, -turned_values], axis=0)
    weights = jnp.concatenate([new_real, new_imag], axis=0)
    return lax.dot_general(weights, stacked, (((0,), (0,)), ((), ())), precision=precise)


def apply_potential(band_coeffs, columns, potential_xyz):
    empty = jnp.zeros((GRID * GRID, GRID), band_coeffs.dtype)
    real_part = empty.at[columns].set(band_coeffs[:, :GRID])
    imag_part = empty.at[columns].set(band_coeffs[:, GRID:])
    field = lax.complex(real_part, imag_part).reshape(GRID, GRID, GRID)
    volume = float(GRID) ** 3
    real_space = jnp.fft.ifftn(field) * volume
    real_space = real_space * potential_xyz
    spectrum = jnp.fft.fftn(real_space) / volume
    spectrum = spectrum.reshape(GRID * GRID, GRID)[columns]
    return jnp.concatenate([jnp.real(spectrum), jnp.imag(spectrum)], axis=1)


def reference(coeffs, columns, potential, ritz_vectors):
    potential_xyz = jnp.transpose(potential.reshape(GRID, GRID, GRID), (1, 2, 0))
    kinetic = kinetic_table(columns, GRID)
    kinetic_both = jnp.concatenate([kinetic, kinetic], axis=1)
    applied = lax.map(lambda band_coeffs: apply_potential(band_coeffs, columns, potential_xyz), coeffs)
    hcoeffs = applied + kinetic_both[None] * coeffs
    norm_total = float(STICKS * GRID)
    flat_coeffs = coeffs.reshape(NB, -1)
    turned = swap_halves(coeffs).reshape(NB, -1)
    flat_hcoeffs = hcoeffs.reshape(NB, -1)
    turned_hcoeffs = swap_halves(hcoeffs).reshape(NB, -1)
    stacked = jnp.concatenate([flat_coeffs, turned, flat_hcoeffs, turned_hcoeffs], axis=0)
    grams = lax.dot_general(flat_coeffs, stacked, (((1,), (1,)), ((), ())), precision=precise) / norm_total
    new_real, new_imag, values = refine(grams[:, :NB], grams[:, NB:2 * NB], grams[:, 2 * NB:3 * NB], grams[:, 3 * NB:], ritz_vectors[0], ritz_vectors[1])
    refined = rotate(flat_coeffs, turned, new_real, new_imag).reshape(coeffs.shape)
    refined_h = rotate(flat_hcoeffs, turned_hcoeffs, new_real, new_imag).reshape(coeffs.shape)
    return refined, refined_h, values
```

```python
import functools

import jax
import jax.numpy as jnp
import ml_dtypes
import numpy as np
from jax import lax
from jax.experimental import pallas as pl
from jax.experimental.pallas import tpu as pltpu
from jax.sharding import PartitionSpec as P

GRID = 112
BANDS = 16
PENCILS = 16
PLANES = 7
STICKS = 512
OWN = 32
RADIUS = 28

f32 = jnp.float32
bf16 = jnp.bfloat16
MESH = pl.DeviceIdType.MESH
NN = (((1,), (0,)), ((), ()))
NT = (((1,), (1,)), ((), ()))


def parts_of(table, count):
    parts = []
    for _ in range(count):
        part = table.astype(ml_dtypes.bfloat16)
        parts.append(part)
        table = table - part.astype(np.float64)
    return np.stack(parts)


def wave_table():
    index = np.arange(GRID)
    angle = 2.0 * np.pi * (np.outer(index, index) % GRID) / GRID
    table = np.zeros((256, 128))
    table[:GRID, :GRID] = np.cos(angle)
    table[128 : 128 + GRID, :GRID] = np.sin(angle)
    return parts_of(table, 3)


def z_tables():
    inverse = np.zeros((64, 4, 256))
    forward = np.zeros((64, 4, 256))
    k = np.arange(GRID)
    for p in range(PENCILS):
        for r in range(4):
            for q in range(4):
                z = 4 * (q % 2) + r
                if z >= PLANES:
                    continue
                angle = 2.0 * np.pi * ((k * (PLANES * p + z)) % GRID) / GRID
                cosine, sine = np.cos(angle), np.sin(angle)
                real = q // 2 == 0
                row = 4 * p + r
                inverse[row, q, :GRID] = cosine if real else sine
                inverse[row, q, 128 : 128 + GRID] = -sine if real else cosine
                forward[row, q, :GRID] = cosine if real else sine
                forward[row, q, 128 : 128 + GRID] = -sine if real else cosine
    return parts_of(inverse.reshape(64, 1024), 2), parts_of(forward.reshape(64, 1024) / float(GRID) ** 3, 2)


def split(x):
    high = x.astype(bf16)
    return high, (x - high.astype(f32)).astype(bf16)


def dot(a, b, dims=NN):
    return lax.dot_general(a, b, dims, preferred_element_type=f32)


def dot3(a, b, dims=NN):
    return dot(a[0], b[0], dims) + dot(a[0], b[1], dims) + dot(a[1], b[0], dims)


def dot_exact(a, b, dims=NN):
    return lax.dot_general(a, b, dims, precision=lax.Precision.HIGHEST, preferred_element_type=f32)


def slot_of(p):
    return lax.rem(p, 4) * 4 + lax.div(p, 4)


def frequency(index):
    return jnp.where(index < GRID // 2, index, index - GRID).astype(f32)


def wide(x):
    lane = lax.broadcasted_iota(jnp.int32, x.shape, 1)
    moved = pltpu.roll(x, 16, 1)
    return jnp.where(lane < GRID, x, jnp.where(lane < 128, 0.0, moved))


def narrow(x):
    lane = lax.broadcasted_iota(jnp.int32, x.shape, 1)
    moved = pltpu.roll(x, 240, 1)
    return jnp.where(lane < GRID, x, moved)


def turned(x):
    return jnp.concatenate([x[:, 128:], -x[:, :128]], axis=1)


def kernel(
    coeffs_ref, columns_ref, potential_ref, ritz_ref, inverse_ref, forward_ref, wave_ref,
    refined_ref, refined_h_ref, values_ref,
    pad_ref, own_ref, block_ref, send_b, recv_b, send_d, recv_d, psi_ref, a_ref, t_ref, v_ref, p_ref, c_ref,
    bands_ref, own_h_ref, bands_h_ref, sums_ref, send_g, recv_g, row_ref, recv_r,
    sem_sb, sem_rb, sem_sd, sem_rd, sem_sp, sem_rp, sem_sh, sem_rh, sem_sg, sem_rg, sem_sr, sem_rr,
):
    pencil = lax.axis_index("pencil")
    band = lax.axis_index("band")

    def pencil_peer(d):
        return lax.rem(pencil + d, PENCILS)

    def band_peer(d):
        return lax.rem(band + d, BANDS)

    def each(body):
        def step(d, carry):
            body(d)
            return carry

        lax.fori_loop(1, 16, step, 0)

    def to_b(p, mine):
        return pltpu.make_async_remote_copy(
            send_b.at[p], recv_b.at[slot_of(mine)], sem_sb.at[p], sem_rb.at[mine],
            device_id=(p, band), device_id_type=MESH,
        )

    def to_d(p, mine):
        return pltpu.make_async_remote_copy(
            send_d.at[slot_of(p)], recv_d.at[mine], sem_sd.at[p], sem_rd.at[mine],
            device_id=(p, band), device_id_type=MESH,
        )

    def to_g(p, mine):
        return pltpu.make_async_remote_copy(
            send_g, recv_g.at[mine], sem_sg.at[p], sem_rg.at[mine], device_id=(p, band), device_id_type=MESH
        )

    def to_p(b, mine):
        return pltpu.make_async_remote_copy(
            own_ref, bands_ref.at[mine], sem_sp.at[b], sem_rp.at[mine], device_id=(pencil, b), device_id_type=MESH
        )

    def to_h(b, mine):
        return pltpu.make_async_remote_copy(
            own_h_ref, bands_h_ref.at[mine], sem_sh.at[b], sem_rh.at[mine], device_id=(pencil, b), device_id_type=MESH
        )

    def to_r(b, mine):
        return pltpu.make_async_remote_copy(
            row_ref, recv_r.at[mine], sem_sr.at[b], sem_rr.at[mine], device_id=(pencil, b), device_id_type=MESH
        )

    barrier = pltpu.get_barrier_semaphore()

    def greet(d):
        pl.semaphore_signal(barrier, inc=1, device_id=(pencil_peer(d), band), device_id_type=MESH)
        pl.semaphore_signal(barrier, inc=1, device_id=(pencil, band_peer(d)), device_id_type=MESH)

    each(greet)

    pad_ref[...] = jnp.zeros_like(pad_ref)
    pad_ref[:, : 2 * GRID] = coeffs_ref[0]
    own = wide(pad_ref[...])
    own_ref[...] = own
    own_high, own_low = split(own)
    block_ref[...] = jnp.zeros_like(block_ref)
    for q in range(4):
        block_ref[0, 32 * q : 32 * q + 32, 256 * q : 256 * q + 256] = own_high
        block_ref[1, 32 * q : 32 * q + 32, 256 * q : 256 * q + 256] = own_low
    packed = dot3((inverse_ref[0], inverse_ref[1]), (block_ref[0], block_ref[1]), NT)
    send_b[...] = packed.reshape(PENCILS, 4, 128)

    pl.semaphore_wait(barrier, 30)
    each(lambda d: to_b(pencil_peer(d), pencil).start())
    each(lambda d: to_p(band_peer(d), band).start())
    recv_b[slot_of(pencil)] = send_b[pencil]
    bands_ref[band] = own

    columns = columns_ref[...]
    index_x = lax.div(columns, GRID)
    index_y = lax.rem(columns, GRID)
    row = lax.broadcasted_iota(jnp.int32, (128, STICKS), 0)
    hot_x = jnp.where(row == index_x, 1.0, 0.0).astype(bf16)
    hot_y = jnp.where(row == index_y, 1.0, 0.0).astype(bf16)
    a_ref[...] = dot(wave_ref[0], hot_x) + dot(wave_ref[1], hot_x) + dot(wave_ref[2], hot_x)
    for part in range(2):
        table = dot(wave_ref[part], hot_y).astype(bf16)
        t_ref[part, :, :STICKS] = table
        t_ref[part, :128, STICKS:] = -table[128:]
        t_ref[part, 128:, STICKS:] = table[:128]
    v_ref[...] = jnp.zeros_like(v_ref)

    def lay_out(g, carry):
        block = potential_ref[:, pl.ds(pl.multiple_of(896 * g, 128), 896)]
        for k in range(8):
            v_ref[8 * g + k, :PLANES, :GRID] = block[:, GRID * k : GRID * k + GRID]
        return carry

    lax.fori_loop(0, 14, lay_out, 0)

    freq_x, freq_y = frequency(index_x), frequency(index_y)
    lateral = freq_x * freq_x + freq_y * freq_y
    stick = lax.broadcasted_iota(jnp.int32, (OWN, STICKS), 1)
    mine = stick == lax.broadcasted_iota(jnp.int32, (OWN, STICKS), 0) + OWN * pencil
    own_lateral = jnp.sum(jnp.where(mine, lateral, 0.0), axis=1, keepdims=True)
    lane = lax.broadcasted_iota(jnp.int32, (OWN, 256), 1)
    freq_z = frequency(jnp.where(lane < 128, lane, lane - 128))
    kinetic = 0.5 * (own_lateral + freq_z * freq_z) / float(RADIUS * RADIUS)

    each(lambda d: to_b(pencil_peer(d), pencil_peer(d)).wait_recv())
    got = recv_b[...].reshape(4, 16, 128)
    group = lax.div(lax.broadcasted_iota(jnp.int32, (16, 128), 1), 32)
    for q in range(4):
        out = got[0] if q == 0 else pltpu.roll(got[0], (-32 * q) % 128, 1)
        for p in range(1, 4):
            moved = got[p] if p == q else pltpu.roll(got[p], (32 * (p - q)) % 128, 1)
            out = jnp.where(group == p, moved, out)
        for t in range(4):
            psi_ref[q // 2, 4 * (q % 2) : 4 * (q % 2) + 4, 128 * t : 128 * t + 128] = out[4 * t : 4 * t + 4]

    psi_r, psi_i = psi_ref[0], psi_ref[1]

    def phases(x):
        return a_ref[pl.ds(x, 1), :], a_ref[pl.ds(128 + x, 1), :]

    def spread(n, carry):
        real, imag = [], []
        for k in range(2):
            a_r, a_i = phases(2 * n + k)
            real.append(a_r * psi_r - a_i * psi_i)
            imag.append(a_r * psi_i + a_i * psi_r)
        rows = pl.ds(pl.multiple_of(16 * n, 16), 16)
        p_ref[0, rows, :STICKS], p_ref[1, rows, :STICKS] = split(jnp.concatenate(real, axis=0))
        p_ref[0, rows, STICKS:], p_ref[1, rows, STICKS:] = split(jnp.concatenate(imag, axis=0))
        return carry

    lax.fori_loop(0, 56, spread, 0)

    def plane_rows(n, carry):
        rows = pl.ds(pl.multiple_of(224 * n, 224), 224)
        u = dot3((p_ref[0, rows, :], p_ref[1, rows, :]), (t_ref[0], t_ref[1]), NT)
        v = v_ref[pl.ds(28 * n, 28)].reshape(224, 128)
        w = u * jnp.concatenate([v, v], axis=1)
        c_ref[rows, :] = dot3(split(w), (t_ref[0], t_ref[1]))
        return carry

    lax.fori_loop(0, 4, plane_rows, 0)

    def collect(n, carry):
        w_r, w_i = carry
        for k in range(4):
            x = 4 * n + k
            a_r, a_i = phases(x)
            rows = pl.ds(pl.multiple_of(8 * x, 8), 8)
            c_r, c_i = c_ref[rows, :STICKS], c_ref[rows, STICKS:]
            w_r = w_r + (a_r * c_r + a_i * c_i)
            w_i = w_i + (a_r * c_i - a_i * c_r)
        return w_r, w_i

    zero = jnp.zeros((8, STICKS), f32)
    sums = lax.fori_loop(0, 28, collect, (zero, zero))

    outs = []
    for q in range(4):
        half = sums[q // 2][4 * (q % 2) : 4 * (q % 2) + 4]
        outs.append(jnp.concatenate([half[:, 128 * t : 128 * t + 128] for t in range(4)], axis=0))
    for p in range(4):
        out = outs[0] if p == 0 else pltpu.roll(outs[0], (-32 * p) % 128, 1)
        for q in range(1, 4):
            moved = outs[q] if p == q else pltpu.roll(outs[q], (32 * (q - p)) % 128, 1)
            out = jnp.where(group == q, moved, out)
        send_d[4 * p : 4 * p + 4] = out.reshape(4, 4, 128)
    each(lambda d: to_d(pencil_peer(d), pencil).start())
    recv_d[pencil] = send_d[slot_of(pencil)]

    pick = lax.broadcasted_iota(jnp.int32, (256, 128), 0)
    ones = jnp.ones((8, 256), f32)

    def gram_row(values, first):
        other = turned(values)

        def one(i, carry):
            member = bands_ref[i]
            real, imag = member * values, member * other
            rows = pl.ds(pl.multiple_of(8 * i, 8), 8)
            later = pl.ds(pl.multiple_of(128 + 8 * i, 8), 8)
            sums_ref[rows, :] = (real[:8] + real[8:16]) + (real[16:24] + real[24:])
            sums_ref[later, :] = (imag[:8] + imag[8:16]) + (imag[16:24] + imag[24:])
            return carry

        lax.fori_loop(0, BANDS, one, 0)
        target = lax.broadcasted_iota(jnp.int32, (256, 128), 1)
        chosen = jnp.where(lax.div(pick, 8) + first == target, 1.0, 0.0)
        return dot_exact(dot_exact(ones, sums_ref[...], NT), chosen)[:1]

    each(lambda d: to_p(band_peer(d), band_peer(d)).wait_recv())
    overlap_row = gram_row(own, 32)

    each(lambda d: to_d(pencil_peer(d), pencil_peer(d)).wait_recv())
    back = split(recv_d[...].reshape(64, 128).T)
    own_h = kinetic * own
    for q in range(4):
        rows, cols = slice(32 * q, 32 * q + 32), slice(256 * q, 256 * q + 256)
        own_h = own_h + dot3(
            (back[0][rows], back[1][rows]), (forward_ref[0, :, cols], forward_ref[1, :, cols])
        )
    own_h_ref[...] = own_h
    each(lambda d: to_h(band_peer(d), band).start())
    bands_h_ref[band] = own_h

    send_g[...] = gram_row(own_h, 0) + overlap_row
    each(lambda d: to_g(pencil_peer(d), pencil).start())
    recv_g[pencil] = send_g[...]
    each(lambda d: to_g(pencil_peer(d), pencil_peer(d)).wait_recv())
    row_ref[...] = jnp.sum(recv_g[...], axis=0) / float(STICKS * GRID)
    each(lambda d: to_r(band_peer(d), band).start())
    recv_r[band] = row_ref[...]

    x_r, x_i = ritz_ref[0], ritz_ref[1]
    xt = jnp.concatenate([x_r.T, x_i.T], axis=1)
    conj = jnp.concatenate(
        [jnp.concatenate([x_r, -x_i], axis=1), jnp.concatenate([x_i, x_r], axis=1)], axis=0
    )
    each(lambda d: to_r(band_peer(d), band_peer(d)).wait_recv())
    grams = recv_r[...].reshape(BANDS, 128)
    lane = lax.broadcasted_iota(jnp.int32, (BANDS, 128), 1)
    swapped = jnp.where(lax.rem(lane, 32) < 16, -pltpu.roll(grams, 112, 1), pltpu.roll(grams, 16, 1))
    half = dot_exact(xt, jnp.concatenate([grams, swapped], axis=0))
    energy = dot_exact(half[:, :32], conj)
    metric = dot_exact(half[:, 32:64], conj)
    row16 = lax.broadcasted_iota(jnp.int32, (BANDS, 16), 0)
    diagonal = row16 == lax.broadcasted_iota(jnp.int32, (BANDS, 16), 1)
    ratio = jnp.where(diagonal, energy[:, :16] / metric[:, :16], 0.0)
    value_j = jnp.sum(ratio, axis=1, keepdims=True)
    value_i = jnp.sum(ratio, axis=0, keepdims=True)
    values_ref[...] = value_i
    spacing = value_j - value_i
    factor = spacing / jnp.maximum(spacing * spacing, (0.25 / BANDS) ** 2)
    residual_r = jnp.where(diagonal, 1.0, 0.0) - metric[:, :16]
    residual_i = -metric[:, 16:]
    update_r = jnp.where(diagonal, 0.5 * residual_r, (energy[:, :16] + value_j * residual_r) * factor)
    update_i = jnp.where(diagonal, 0.5 * residual_i, (energy[:, 16:] + value_j * residual_i) * factor)
    chosen = row16 == band
    u_r = jnp.sum(jnp.where(chosen, update_r + jnp.where(diagonal, 1.0, 0.0), 0.0), axis=0, keepdims=True)
    u_i = jnp.sum(jnp.where(chosen, update_i, 0.0), axis=0, keepdims=True)
    new_r = jnp.sum(x_r * u_r - x_i * u_i, axis=1, keepdims=True)
    new_i = jnp.sum(x_r * u_i + x_i * u_r, axis=1, keepdims=True)

    def rotate(members):
        along = jnp.zeros((OWN, 256), f32)
        across = jnp.zeros((OWN, 256), f32)
        for i in range(BANDS):
            member = members[i]
            along = along + new_r[i : i + 1] * member
            across = across + new_i[i : i + 1] * member
        return narrow(along - turned(across))[:, : 2 * GRID]

    refined_ref[0] = rotate(bands_ref)
    each(lambda d: to_h(band_peer(d), band_peer(d)).wait_recv())
    refined_h_ref[0] = rotate(bands_h_ref)

    def finish(d):
        to_b(pencil_peer(d), pencil).wait_send()
        to_d(pencil_peer(d), pencil).wait_send()
        to_g(pencil_peer(d), pencil).wait_send()
        to_p(band_peer(d), band).wait_send()
        to_h(band_peer(d), band).wait_send()
        to_r(band_peer(d), band).wait_send()

    each(finish)


def shards(coeffs, columns, potential, ritz_vectors):
    inverse, forward = z_tables()
    vmem = pl.BlockSpec(memory_space=pltpu.VMEM)
    refined, refined_h, values = pl.pallas_call(
        kernel,
        out_shape=(
            jax.ShapeDtypeStruct((1, OWN, 2 * GRID), f32),
            jax.ShapeDtypeStruct((1, OWN, 2 * GRID), f32),
            jax.ShapeDtypeStruct((1, BANDS), f32),
        ),
        in_specs=[vmem] * 7,
        out_specs=(vmem,) * 3,
        scratch_shapes=[
            pltpu.VMEM((OWN, 256), f32),
            pltpu.VMEM((OWN, 256), f32),
            pltpu.VMEM((2, 128, 1024), bf16),
            pltpu.VMEM((16, 4, 128), f32),
            pltpu.VMEM((16, 4, 128), f32),
            pltpu.VMEM((16, 4, 128), f32),
            pltpu.VMEM((16, 4, 128), f32),
            pltpu.VMEM((2, 8, STICKS), f32),
            pltpu.VMEM((256, STICKS), f32),
            pltpu.VMEM((2, 256, 1024), bf16),
            pltpu.VMEM((GRID, 8, 128), f32),
            pltpu.VMEM((2, 896, 1024), bf16),
            pltpu.VMEM((896, 1024), f32),
            pltpu.VMEM((BANDS, OWN, 256), f32),
            pltpu.VMEM((OWN, 256), f32),
            pltpu.VMEM((BANDS, OWN, 256), f32),
            pltpu.VMEM((256, 256), f32),
            pltpu.VMEM((1, 128), f32),
            pltpu.VMEM((16, 1, 128), f32),
            pltpu.VMEM((1, 128), f32),
            pltpu.VMEM((16, 1, 128), f32),
        ]
        + [pltpu.SemaphoreType.DMA((16,))] * 12,
        compiler_params=pltpu.CompilerParams(
            collective_id=0, has_side_effects=True, vmem_limit_bytes=48 * 2**20
        ),
    )(
        coeffs,
        columns.reshape(1, STICKS),
        potential,
        ritz_vectors,
        jnp.asarray(inverse),
        jnp.asarray(forward),
        jnp.asarray(wave_table()),
    )
    return refined, refined_h, values.reshape(BANDS)


def solution(mesh):
    return jax.shard_map(
        shards,
        mesh=mesh,
        in_specs=(P("band", "pencil", None), P(), P("pencil", None), P()),
        out_specs=(P("band", "pencil", None), P("band", "pencil", None), P()),
        check_vma=False,
    )
```

```python
import functools

import jax
import jax.numpy as jnp
import ml_dtypes
import numpy as np
from jax import lax
from jax.experimental import pallas as pl
from jax.experimental.pallas import tpu as pltpu
from jax.sharding import PartitionSpec as P

GRID = 112
BANDS = 16
PENCILS = 16
PLANES = 7
STICKS = 512
OWN = 32
RADIUS = 28

f32 = jnp.float32
bf16 = jnp.bfloat16
MESH = pl.DeviceIdType.MESH
NN = (((1,), (0,)), ((), ()))
NT = (((1,), (1,)), ((), ()))


def parts_of(table, count):
    parts = []
    for _ in range(count):
        part = table.astype(ml_dtypes.bfloat16)
        parts.append(part)
        table = table - part.astype(np.float64)
    return np.stack(parts)


def wave_table():
    index = np.arange(GRID)
    angle = 2.0 * np.pi * (np.outer(index, index) % GRID) / GRID
    table = np.zeros((256, 128))
    table[:GRID, :GRID] = np.cos(angle)
    table[128 : 128 + GRID, :GRID] = np.sin(angle)
    return parts_of(table, 3)


def z_tables():
    inverse = np.zeros((64, 4, 256))
    forward = np.zeros((64, 4, 256))
    k = np.arange(GRID)
    for p in range(PENCILS):
        for r in range(4):
            for q in range(4):
                z = 4 * (q % 2) + r
                if z >= PLANES:
                    continue
                angle = 2.0 * np.pi * ((k * (PLANES * p + z)) % GRID) / GRID
                cosine, sine = np.cos(angle), np.sin(angle)
                real = q // 2 == 0
                row = 4 * p + r
                inverse[row, q, :GRID] = cosine if real else sine
                inverse[row, q, 128 : 128 + GRID] = -sine if real else cosine
                forward[row, q, :GRID] = cosine if real else sine
                forward[row, q, 128 : 128 + GRID] = -sine if real else cosine
    return parts_of(inverse.reshape(64, 1024), 2), parts_of(forward.reshape(64, 1024) / float(GRID) ** 3, 2)


def split(x):
    high = x.astype(bf16)
    return high, (x - high.astype(f32)).astype(bf16)


def dot(a, b, dims=NN):
    return lax.dot_general(a, b, dims, preferred_element_type=f32)


def dot3(a, b, dims=NN):
    return dot(a[0], b[0], dims) + dot(a[0], b[1], dims) + dot(a[1], b[0], dims)


def dot_exact(a, b, dims=NN):
    return lax.dot_general(a, b, dims, precision=lax.Precision.HIGHEST, preferred_element_type=f32)


def slot_of(p):
    return lax.rem(p, 4) * 4 + lax.div(p, 4)


def frequency(index):
    return jnp.where(index < GRID // 2, index, index - GRID).astype(f32)


def wide(x):
    lane = lax.broadcasted_iota(jnp.int32, x.shape, 1)
    moved = pltpu.roll(x, 16, 1)
    return jnp.where(lane < GRID, x, jnp.where(lane < 128, 0.0, moved))


def narrow(x):
    lane = lax.broadcasted_iota(jnp.int32, x.shape, 1)
    moved = pltpu.roll(x, 240, 1)
    return jnp.where(lane < GRID, x, moved)


def turned(x):
    return jnp.concatenate([x[:, 128:], -x[:, :128]], axis=1)


def kernel(
    coeffs_hbm, columns_hbm, potential_hbm, ritz_hbm, inverse_hbm, forward_hbm, wave_hbm,
    refined_ref, refined_h_ref, values_ref,
    coeffs_ref, columns_ref, potential_ref, ritz_ref, inverse_ref, forward_ref, wave_ref, sem_in,
    pad_ref, block_ref, send_b, recv_b, send_d, recv_d, psi_ref, a_ref, t_ref, v_ref, p_ref, w_ref, c_ref,
    bands_ref, bands_h_ref, sums_ref, send_g, recv_g, row_ref, recv_r,
    sem_sb, sem_rb, sem_sd, sem_rd, sem_sp, sem_fp, sem_rp, sem_sh, sem_fh, sem_rh, sem_sg, sem_rg, sem_sr, sem_rr,
):
    pencil = lax.axis_index("pencil")
    band = lax.axis_index("band")

    def pencil_peer(d):
        return lax.rem(pencil + d, PENCILS)

    def band_peer(d):
        return lax.rem(band + d, BANDS)

    def each(body):
        def step(d, carry):
            body(d)
            return carry

        lax.fori_loop(1, 16, step, 0)

    def to_b(p, mine):
        return pltpu.make_async_remote_copy(
            send_b.at[p], recv_b.at[slot_of(mine)], sem_sb.at[p], sem_rb.at[mine],
            device_id=(p, band), device_id_type=MESH,
        )

    def to_d(p, mine):
        return pltpu.make_async_remote_copy(
            send_d.at[slot_of(p)], recv_d.at[mine], sem_sd.at[p], sem_rd.at[mine],
            device_id=(p, band), device_id_type=MESH,
        )

    def to_g(p, mine):
        return pltpu.make_async_remote_copy(
            send_g, recv_g.at[mine], sem_sg.at[p], sem_rg.at[mine], device_id=(p, band), device_id_type=MESH
        )

    sibling = band + 1 - 2 * lax.rem(band, 2)

    def chip_peer(d):
        return lax.rem(band + 2 * d, BANDS)

    def to_p(b, mine):
        return pltpu.make_async_remote_copy(
            bands_ref.at[mine], bands_ref.at[mine], sem_sp.at[b], sem_rp.at[mine],
            device_id=(pencil, b), device_id_type=MESH,
        )

    def hand_p(q):
        return pltpu.make_async_remote_copy(
            bands_ref.at[q], bands_ref.at[q], sem_fp.at[q], sem_rp.at[q],
            device_id=(pencil, sibling), device_id_type=MESH,
        )

    def to_h(b, mine):
        return pltpu.make_async_remote_copy(
            bands_h_ref.at[mine], bands_h_ref.at[mine], sem_sh.at[b], sem_rh.at[mine],
            device_id=(pencil, b), device_id_type=MESH,
        )

    def hand_h(q):
        return pltpu.make_async_remote_copy(
            bands_h_ref.at[q], bands_h_ref.at[q], sem_fh.at[q], sem_rh.at[q],
            device_id=(pencil, sibling), device_id_type=MESH,
        )

    def chips(body, first=1):
        def step(d, carry):
            body(d)
            return carry

        lax.fori_loop(first, 8, step, 0)

    def to_r(b, mine):
        return pltpu.make_async_remote_copy(
            row_ref, recv_r.at[mine], sem_sr.at[b], sem_rr.at[mine], device_id=(pencil, b), device_id_type=MESH
        )

    sources = (coeffs_hbm, inverse_hbm, columns_hbm, wave_hbm, potential_hbm, forward_hbm, ritz_hbm)
    targets = (coeffs_ref, inverse_ref, columns_ref, wave_ref, potential_ref, forward_ref, ritz_ref)
    loads = [pltpu.make_async_copy(a, b, sem_in.at[k]) for k, (a, b) in enumerate(zip(sources, targets))]
    barrier = pltpu.get_barrier_semaphore()
    for load in loads[:2]:
        load.start()

    def greet(d):
        pl.semaphore_signal(barrier, inc=1, device_id=(pencil_peer(d), band), device_id_type=MESH)
        pl.semaphore_signal(barrier, inc=1, device_id=(pencil, band_peer(d)), device_id_type=MESH)

    each(greet)
    for load in loads[2:]:
        load.start()
    for load in loads[:2]:
        load.wait()

    pad_ref[...] = jnp.zeros_like(pad_ref)
    pad_ref[:, : 2 * GRID] = coeffs_ref[0]
    own = wide(pad_ref[...])
    bands_ref[band] = own
    own_high, own_low = split(own)
    block_ref[...] = jnp.zeros_like(block_ref)
    for q in range(4):
        block_ref[0, 32 * q : 32 * q + 32, 256 * q : 256 * q + 256] = own_high
        block_ref[1, 32 * q : 32 * q + 32, 256 * q : 256 * q + 256] = own_low
    packed = dot3((inverse_ref[0], inverse_ref[1]), (block_ref[0], block_ref[1]), NT)
    send_b[...] = packed.reshape(PENCILS, 4, 128)

    pl.semaphore_wait(barrier, 30)
    each(lambda d: to_b(pencil_peer(d), pencil).start())
    chips(lambda d: to_p(chip_peer(d), band).start())
    hand_p(band).start()
    recv_b[slot_of(pencil)] = send_b[pencil]
    for load in loads[2:]:
        load.wait()

    columns = columns_ref[...]
    index_x = lax.div(columns, GRID)
    index_y = lax.rem(columns, GRID)
    row = lax.broadcasted_iota(jnp.int32, (128, STICKS), 0)
    hot_x = jnp.where(row == index_x, 1.0, 0.0).astype(bf16)
    hot_y = jnp.where(row == index_y, 1.0, 0.0).astype(bf16)
    a_ref[...] = dot(wave_ref[0], hot_x) + dot(wave_ref[1], hot_x) + dot(wave_ref[2], hot_x)
    for part in range(2):
        table = dot(wave_ref[part], hot_y).astype(bf16)
        t_ref[part, :, :STICKS] = table
        t_ref[part, :128, STICKS:] = -table[128:]
        t_ref[part, 128:, STICKS:] = table[:128]
    v_ref[...] = jnp.zeros_like(v_ref)

    def lay_out(g, carry):
        block = potential_ref[:, pl.ds(pl.multiple_of(896 * g, 128), 896)]
        for k in range(8):
            v_ref[8 * g + k, :PLANES, :GRID] = block[:, GRID * k : GRID * k + GRID]
        return carry

    lax.fori_loop(0, 14, lay_out, 0)

    freq_x, freq_y = frequency(index_x), frequency(index_y)
    lateral = freq_x * freq_x + freq_y * freq_y
    stick = lax.broadcasted_iota(jnp.int32, (OWN, STICKS), 1)
    mine = stick == lax.broadcasted_iota(jnp.int32, (OWN, STICKS), 0) + OWN * pencil
    own_lateral = jnp.sum(jnp.where(mine, lateral, 0.0), axis=1, keepdims=True)
    lane = lax.broadcasted_iota(jnp.int32, (OWN, 256), 1)
    freq_z = frequency(jnp.where(lane < 128, lane, lane - 128))
    kinetic = 0.5 * (own_lateral + freq_z * freq_z) / float(RADIUS * RADIUS)

    each(lambda d: to_b(pencil_peer(d), pencil_peer(d)).wait_recv())
    got = recv_b[...].reshape(4, 16, 128)
    group = lax.div(lax.broadcasted_iota(jnp.int32, (16, 128), 1), 32)
    for q in range(4):
        out = got[0] if q == 0 else pltpu.roll(got[0], (-32 * q) % 128, 1)
        for p in range(1, 4):
            moved = got[p] if p == q else pltpu.roll(got[p], (32 * (p - q)) % 128, 1)
            out = jnp.where(group == p, moved, out)
        for t in range(4):
            psi_ref[q // 2, 4 * (q % 2) : 4 * (q % 2) + 4, 128 * t : 128 * t + 128] = out[4 * t : 4 * t + 4]

    psi_r, psi_i = psi_ref[0], psi_ref[1]

    def phases(x):
        return a_ref[pl.ds(x, 1), :], a_ref[pl.ds(128 + x, 1), :]

    def spread(n, carry):
        real, imag = [], []
        for k in range(2):
            a_r, a_i = phases(2 * n + k)
            real.append(a_r * psi_r - a_i * psi_i)
            imag.append(a_r * psi_i + a_i * psi_r)
        rows = pl.ds(pl.multiple_of(16 * n, 16), 16)
        p_ref[0, rows, :STICKS], p_ref[1, rows, :STICKS] = split(jnp.concatenate(real, axis=0))
        p_ref[0, rows, STICKS:], p_ref[1, rows, STICKS:] = split(jnp.concatenate(imag, axis=0))
        return carry

    lax.fori_loop(0, 56, spread, 0)

    u = dot3((p_ref[0], p_ref[1]), (t_ref[0], t_ref[1]), NT)
    v = v_ref[...].reshape(896, 128)
    for part in range(2):
        cols = slice(128 * part, 128 * part + 128)
        w_ref[0, :, cols], w_ref[1, :, cols] = split(u[:, cols] * v)

    def back_rows(n, carry):
        rows = pl.ds(pl.multiple_of(448 * n, 448), 448)
        c_ref[rows, :] = dot3((w_ref[0, rows, :], w_ref[1, rows, :]), (t_ref[0], t_ref[1]))
        return carry

    lax.fori_loop(0, 2, back_rows, 0)

    def collect(n, carry):
        w_r, w_i = carry
        for k in range(4):
            x = 4 * n + k
            a_r, a_i = phases(x)
            rows = pl.ds(pl.multiple_of(8 * x, 8), 8)
            c_r, c_i = c_ref[rows, :STICKS], c_ref[rows, STICKS:]
            w_r = w_r + (a_r * c_r + a_i * c_i)
            w_i = w_i + (a_r * c_i - a_i * c_r)
        return w_r, w_i

    zero = jnp.zeros((8, STICKS), f32)
    sums = lax.fori_loop(0, 28, collect, (zero, zero))

    outs = []
    for q in range(4):
        half = sums[q // 2][4 * (q % 2) : 4 * (q % 2) + 4]
        outs.append(jnp.concatenate([half[:, 128 * t : 128 * t + 128] for t in range(4)], axis=0))
    for p in range(4):
        out = outs[0] if p == 0 else pltpu.roll(outs[0], (-32 * p) % 128, 1)
        for q in range(1, 4):
            moved = outs[q] if p == q else pltpu.roll(outs[q], (32 * (q - p)) % 128, 1)
            out = jnp.where(group == q, moved, out)
        send_d[4 * p : 4 * p + 4] = out.reshape(4, 4, 128)
    each(lambda d: to_d(pencil_peer(d), pencil).start())
    recv_d[pencil] = send_d[slot_of(pencil)]

    pick = lax.broadcasted_iota(jnp.int32, (256, 128), 0)
    ones = jnp.ones((8, 256), f32)

    def gram_row(values, first):
        other = turned(values)

        def one(i, carry):
            member = bands_ref[i]
            real, imag = member * values, member * other
            rows = pl.ds(pl.multiple_of(8 * i, 8), 8)
            later = pl.ds(pl.multiple_of(128 + 8 * i, 8), 8)
            sums_ref[rows, :] = (real[:8] + real[8:16]) + (real[16:24] + real[24:])
            sums_ref[later, :] = (imag[:8] + imag[8:16]) + (imag[16:24] + imag[24:])
            return carry

        lax.fori_loop(0, BANDS, one, 0)
        target = lax.broadcasted_iota(jnp.int32, (256, 128), 1)
        chosen = jnp.where(lax.div(pick, 8) + first == target, 1.0, 0.0)
        return dot_exact(dot_exact(ones, sums_ref[...], NT), chosen)[:1]

    def hand_on_p(d):
        to_p(chip_peer(d), chip_peer(d)).wait_recv()
        hand_p(chip_peer(d)).start()

    chips(hand_on_p)
    chips(lambda d: hand_p(lax.rem(sibling + 2 * d, BANDS)).wait_recv(), 0)
    overlap_row = gram_row(own, 32)

    each(lambda d: to_d(pencil_peer(d), pencil_peer(d)).wait_recv())
    back = split(recv_d[...].reshape(64, 128).T)
    own_h = kinetic * own
    for q in range(4):
        rows, cols = slice(32 * q, 32 * q + 32), slice(256 * q, 256 * q + 256)
        own_h = own_h + dot3(
            (back[0][rows], back[1][rows]), (forward_ref[0, :, cols], forward_ref[1, :, cols])
        )
    bands_h_ref[band] = own_h
    chips(lambda d: to_h(chip_peer(d), band).start())
    hand_h(band).start()

    send_g[...] = gram_row(own_h, 0) + overlap_row
    each(lambda d: to_g(pencil_peer(d), pencil).start())
    recv_g[pencil] = send_g[...]
    each(lambda d: to_g(pencil_peer(d), pencil_peer(d)).wait_recv())
    row_ref[...] = jnp.sum(recv_g[...], axis=0) / float(STICKS * GRID)
    each(lambda d: to_r(band_peer(d), band).start())
    recv_r[band] = row_ref[...]
    for d in (1, 7, 2, 6, 3, 5, 4):
        to_h(chip_peer(d), chip_peer(d)).wait_recv()
        hand_h(chip_peer(d)).start()

    x_r, x_i = ritz_ref[0], ritz_ref[1]
    xt = jnp.concatenate([x_r.T, x_i.T], axis=1)
    conj = jnp.concatenate(
        [jnp.concatenate([x_r, -x_i], axis=1), jnp.concatenate([x_i, x_r], axis=1)], axis=0
    )
    each(lambda d: to_r(band_peer(d), band_peer(d)).wait_recv())
    grams = recv_r[...].reshape(BANDS, 128)
    lane = lax.broadcasted_iota(jnp.int32, (BANDS, 128), 1)
    swapped = jnp.where(lax.rem(lane, 32) < 16, -pltpu.roll(grams, 112, 1), pltpu.roll(grams, 16, 1))
    half = dot_exact(xt, jnp.concatenate([grams, swapped], axis=0))
    energy = dot_exact(half[:, :32], conj)
    metric = dot_exact(half[:, 32:64], conj)
    row16 = lax.broadcasted_iota(jnp.int32, (BANDS, 16), 0)
    diagonal = row16 == lax.broadcasted_iota(jnp.int32, (BANDS, 16), 1)
    ratio = jnp.where(diagonal, energy[:, :16] / metric[:, :16], 0.0)
    value_j = jnp.sum(ratio, axis=1, keepdims=True)
    value_i = jnp.sum(ratio, axis=0, keepdims=True)
    values_ref[...] = value_i
    spacing = value_j - value_i
    factor = spacing / jnp.maximum(spacing * spacing, (0.25 / BANDS) ** 2)
    residual_r = jnp.where(diagonal, 1.0, 0.0) - metric[:, :16]
    residual_i = -metric[:, 16:]
    update_r = jnp.where(diagonal, 0.5 * residual_r, (energy[:, :16] + value_j * residual_r) * factor)
    update_i = jnp.where(diagonal, 0.5 * residual_i, (energy[:, 16:] + value_j * residual_i) * factor)
    chosen = row16 == band
    u_r = jnp.sum(jnp.where(chosen, update_r + jnp.where(diagonal, 1.0, 0.0), 0.0), axis=0, keepdims=True)
    u_i = jnp.sum(jnp.where(chosen, update_i, 0.0), axis=0, keepdims=True)
    new_r = jnp.sum(x_r * u_r - x_i * u_i, axis=1, keepdims=True)
    new_i = jnp.sum(x_r * u_i + x_i * u_r, axis=1, keepdims=True)

    def rotate(members):
        along = jnp.zeros((OWN, 256), f32)
        across = jnp.zeros((OWN, 256), f32)
        for i in range(BANDS):
            member = members[i]
            along = along + new_r[i : i + 1] * member
            across = across + new_i[i : i + 1] * member
        return narrow(along - turned(across))[:, : 2 * GRID]

    refined_ref[0] = rotate(bands_ref)
    chips(lambda d: hand_h(lax.rem(sibling + 2 * d, BANDS)).wait_recv(), 0)
    refined_h_ref[0] = rotate(bands_h_ref)

    def finish(d):
        to_b(pencil_peer(d), pencil).wait_send()
        to_d(pencil_peer(d), pencil).wait_send()
        to_g(pencil_peer(d), pencil).wait_send()
        to_r(band_peer(d), band).wait_send()

    each(finish)
    chips(lambda d: to_p(chip_peer(d), band).wait_send())
    chips(lambda d: to_h(chip_peer(d), band).wait_send())
    chips(lambda d: hand_p(chip_peer(d)).wait_send(), 0)
    chips(lambda d: hand_h(chip_peer(d)).wait_send(), 0)


def emit(*refs):
    sem = refs[6]
    copies = [pltpu.make_async_copy(refs[k], refs[3 + k], sem.at[k]) for k in range(3)]
    for copy in copies:
        copy.start()
    for copy in copies:
        copy.wait()


def shards(coeffs, columns, potential, ritz_vectors):
    inverse, forward = z_tables()
    vmem = pl.BlockSpec(memory_space=pltpu.VMEM)
    outs = (
        jax.ShapeDtypeStruct((1, OWN, 2 * GRID), f32),
        jax.ShapeDtypeStruct((1, OWN, 2 * GRID), f32),
        jax.ShapeDtypeStruct((1, BANDS), f32),
    )
    results = pl.pallas_call(
        kernel,
        out_shape=outs,
        in_specs=[pl.BlockSpec(memory_space=pltpu.HBM)] * 7,
        out_specs=(vmem,) * 3,
        scratch_shapes=[
            pltpu.VMEM((1, OWN, 2 * GRID), f32),
            pltpu.VMEM((1, STICKS), jnp.int32),
            pltpu.VMEM((PLANES, GRID * GRID), f32),
            pltpu.VMEM((2, BANDS, BANDS), f32),
            pltpu.VMEM((2, 64, 1024), bf16),
            pltpu.VMEM((2, 64, 1024), bf16),
            pltpu.VMEM((3, 256, 128), bf16),
            pltpu.SemaphoreType.DMA((7,)),
            pltpu.VMEM((OWN, 256), f32),
            pltpu.VMEM((2, 128, 1024), bf16),
            pltpu.VMEM((16, 4, 128), f32),
            pltpu.VMEM((16, 4, 128), f32),
            pltpu.VMEM((16, 4, 128), f32),
            pltpu.VMEM((16, 4, 128), f32),
            pltpu.VMEM((2, 8, STICKS), f32),
            pltpu.VMEM((256, STICKS), f32),
            pltpu.VMEM((2, 256, 1024), bf16),
            pltpu.VMEM((GRID, 8, 128), f32),
            pltpu.VMEM((2, 896, 1024), bf16),
            pltpu.VMEM((2, 896, 256), bf16),
            pltpu.VMEM((896, 1024), f32),
            pltpu.VMEM((BANDS, OWN, 256), f32),
            pltpu.VMEM((BANDS, OWN, 256), f32),
            pltpu.VMEM((256, 256), f32),
            pltpu.VMEM((1, 128), f32),
            pltpu.VMEM((16, 1, 128), f32),
            pltpu.VMEM((1, 128), f32),
            pltpu.VMEM((16, 1, 128), f32),
        ]
        + [pltpu.SemaphoreType.DMA((16,))] * 14,
        compiler_params=pltpu.CompilerParams(
            collective_id=0, has_side_effects=True, vmem_limit_bytes=62 * 2**20
        ),
    )(
        coeffs,
        columns.reshape(1, STICKS),
        potential,
        ritz_vectors,
        jnp.asarray(inverse),
        jnp.asarray(forward),
        jnp.asarray(wave_table()),
    )
    anywhere = pl.BlockSpec(memory_space=pl.ANY)
    refined, refined_h, values = pl.pallas_call(
        emit,
        out_shape=outs,
        in_specs=[anywhere] * 3,
        out_specs=(anywhere,) * 3,
        scratch_shapes=[pltpu.SemaphoreType.DMA((3,))],
    )(*results)
    return refined, refined_h, values.reshape(BANDS)


def solution(mesh):
    return jax.shard_map(
        shards,
        mesh=mesh,
        in_specs=(P("band", "pencil", None), P(), P("pencil", None), P()),
        out_specs=(P("band", "pencil", None), P("band", "pencil", None), P()),
        check_vma=False,
    )
```

```python
import functools

import jax
import jax.numpy as jnp
import ml_dtypes
import numpy as np
from jax import lax
from jax.experimental import pallas as pl
from jax.experimental.pallas import tpu as pltpu
from jax.sharding import PartitionSpec as P

GRID = 112
BANDS = 16
PENCILS = 16
PLANES = 7
STICKS = 512
OWN = 32
RADIUS = 28

f32 = jnp.float32
bf16 = jnp.bfloat16
MESH = pl.DeviceIdType.MESH
NN = (((1,), (0,)), ((), ()))
NT = (((1,), (1,)), ((), ()))


def parts_of(table, count):
    parts = []
    for _ in range(count):
        part = table.astype(ml_dtypes.bfloat16)
        parts.append(part)
        table = table - part.astype(np.float64)
    return np.stack(parts)


def wave_table():
    index = np.arange(GRID)
    angle = 2.0 * np.pi * (np.outer(index, index) % GRID) / GRID
    table = np.zeros((256, 128))
    table[:GRID, :GRID] = np.cos(angle)
    table[128 : 128 + GRID, :GRID] = np.sin(angle)
    return parts_of(table, 3)


def z_tables():
    inverse = np.zeros((64, 4, 256))
    forward = np.zeros((64, 4, 256))
    k = np.arange(GRID)
    for p in range(PENCILS):
        for r in range(4):
            for q in range(4):
                z = 4 * (q % 2) + r
                if z >= PLANES:
                    continue
                angle = 2.0 * np.pi * ((k * (PLANES * p + z)) % GRID) / GRID
                cosine, sine = np.cos(angle), np.sin(angle)
                real = q // 2 == 0
                row = 4 * p + r
                inverse[row, q, :GRID] = cosine if real else sine
                inverse[row, q, 128 : 128 + GRID] = -sine if real else cosine
                forward[row, q, :GRID] = cosine if real else sine
                forward[row, q, 128 : 128 + GRID] = -sine if real else cosine
    return parts_of(inverse.reshape(64, 1024), 2), parts_of(forward.reshape(64, 1024) / float(GRID) ** 3, 2)


def split(x):
    high = x.astype(bf16)
    return high, (x - high.astype(f32)).astype(bf16)


def dot(a, b, dims=NN):
    return lax.dot_general(a, b, dims, preferred_element_type=f32)


def dot3(a, b, dims=NN):
    return dot(a[0], b[0], dims) + dot(a[0], b[1], dims) + dot(a[1], b[0], dims)


def dot_exact(a, b, dims=NN):
    return lax.dot_general(a, b, dims, precision=lax.Precision.HIGHEST, preferred_element_type=f32)


def slot_of(p):
    return lax.rem(p, 4) * 4 + lax.div(p, 4)


def frequency(index):
    return jnp.where(index < GRID // 2, index, index - GRID).astype(f32)


def wide(x):
    lane = lax.broadcasted_iota(jnp.int32, x.shape, 1)
    moved = pltpu.roll(x, 16, 1)
    return jnp.where(lane < GRID, x, jnp.where(lane < 128, 0.0, moved))


def narrow(x):
    lane = lax.broadcasted_iota(jnp.int32, x.shape, 1)
    moved = pltpu.roll(x, 240, 1)
    return jnp.where(lane < GRID, x, moved)


def turned(x):
    return jnp.concatenate([x[:, 128:], -x[:, :128]], axis=1)


def kernel(
    coeffs_hbm, columns_hbm, potential_hbm, ritz_hbm, inverse_hbm, forward_hbm, wave_hbm,
    refined_ref, refined_h_ref, values_ref,
    coeffs_ref, columns_ref, potential_ref, ritz_ref, inverse_ref, forward_ref, wave_ref, sem_in,
    pad_ref, block_ref, send_b, recv_b, send_d, recv_d, psi_ref, a_ref, t_ref, v_ref, p_ref, w_ref, c_ref,
    bands_ref, bands_h_ref, sums_ref, send_g, recv_g, row_ref, recv_r,
    sem_sb, sem_rb, sem_sd, sem_rd, sem_sp, sem_fp, sem_rp, sem_sh, sem_fh, sem_rh, sem_sg, sem_rg, sem_sr, sem_rr,
):
    pencil = lax.axis_index("pencil")
    band = lax.axis_index("band")

    def pencil_peer(d):
        return lax.rem(pencil + d, PENCILS)

    def band_peer(d):
        return lax.rem(band + d, BANDS)

    def each(body):
        def step(d, carry):
            body(d)
            return carry

        lax.fori_loop(1, 16, step, 0)

    def to_b(p, mine):
        return pltpu.make_async_remote_copy(
            send_b.at[p], recv_b.at[slot_of(mine)], sem_sb.at[p], sem_rb.at[mine],
            device_id=(p, band), device_id_type=MESH,
        )

    def to_d(p, mine):
        return pltpu.make_async_remote_copy(
            send_d.at[slot_of(p)], recv_d.at[mine], sem_sd.at[p], sem_rd.at[mine],
            device_id=(p, band), device_id_type=MESH,
        )

    def to_g(p, mine):
        return pltpu.make_async_remote_copy(
            send_g, recv_g.at[mine], sem_sg.at[p], sem_rg.at[mine], device_id=(p, band), device_id_type=MESH
        )

    sibling = band + 1 - 2 * lax.rem(band, 2)

    def chip_peer(d):
        return lax.rem(band + 2 * d, BANDS)

    def to_p(b, mine):
        return pltpu.make_async_remote_copy(
            bands_ref.at[mine], bands_ref.at[mine], sem_sp.at[b], sem_rp.at[mine],
            device_id=(pencil, b), device_id_type=MESH,
        )

    def hand_p(q):
        return pltpu.make_async_remote_copy(
            bands_ref.at[q], bands_ref.at[q], sem_fp.at[q], sem_rp.at[q],
            device_id=(pencil, sibling), device_id_type=MESH,
        )

    def to_h(b, mine):
        return pltpu.make_async_remote_copy(
            bands_h_ref.at[mine], bands_h_ref.at[mine], sem_sh.at[b], sem_rh.at[mine],
            device_id=(pencil, b), device_id_type=MESH,
        )

    def hand_h(q):
        return pltpu.make_async_remote_copy(
            bands_h_ref.at[q], bands_h_ref.at[q], sem_fh.at[q], sem_rh.at[q],
            device_id=(pencil, sibling), device_id_type=MESH,
        )

    def chips(body, first=1):
        def step(d, carry):
            body(d)
            return carry

        lax.fori_loop(first, 8, step, 0)

    def to_r(b, mine):
        return pltpu.make_async_remote_copy(
            row_ref, recv_r.at[mine], sem_sr.at[b], sem_rr.at[mine], device_id=(pencil, b), device_id_type=MESH
        )

    sources = (coeffs_hbm, inverse_hbm, columns_hbm, wave_hbm, potential_hbm, forward_hbm, ritz_hbm)
    targets = (coeffs_ref, inverse_ref, columns_ref, wave_ref, potential_ref, forward_ref, ritz_ref)
    loads = [pltpu.make_async_copy(a, b, sem_in.at[k]) for k, (a, b) in enumerate(zip(sources, targets))]
    barrier = pltpu.get_barrier_semaphore()
    for load in loads[:2]:
        load.start()

    def greet(d):
        pl.semaphore_signal(barrier, inc=1, device_id=(pencil_peer(d), band), device_id_type=MESH)
        pl.semaphore_signal(barrier, inc=1, device_id=(pencil, band_peer(d)), device_id_type=MESH)

    each(greet)
    for load in loads[2:]:
        load.start()
    for load in loads[:2]:
        load.wait()

    pad_ref[...] = jnp.zeros_like(pad_ref)
    pad_ref[:, : 2 * GRID] = coeffs_ref[0]
    own = wide(pad_ref[...])
    bands_ref[band] = own
    own_high, own_low = split(own)
    block_ref[...] = jnp.zeros_like(block_ref)
    for q in range(4):
        block_ref[0, 32 * q : 32 * q + 32, 256 * q : 256 * q + 256] = own_high
        block_ref[1, 32 * q : 32 * q + 32, 256 * q : 256 * q + 256] = own_low
    packed = dot3((inverse_ref[0], inverse_ref[1]), (block_ref[0], block_ref[1]), NT)
    send_b[...] = packed.reshape(PENCILS, 4, 128)

    pl.semaphore_wait(barrier, 30)
    each(lambda d: to_b(pencil_peer(d), pencil).start())
    chips(lambda d: to_p(chip_peer(d), band).start())
    hand_p(band).start()
    recv_b[slot_of(pencil)] = send_b[pencil]
    for load in loads[2:]:
        load.wait()

    columns = columns_ref[...]
    index_x = lax.div(columns, GRID)
    index_y = lax.rem(columns, GRID)
    row = lax.broadcasted_iota(jnp.int32, (128, STICKS), 0)
    hot_x = jnp.where(row == index_x, 1.0, 0.0).astype(bf16)
    hot_y = jnp.where(row == index_y, 1.0, 0.0).astype(bf16)
    a_ref[...] = dot(wave_ref[0], hot_x) + dot(wave_ref[1], hot_x) + dot(wave_ref[2], hot_x)
    for part in range(2):
        table = dot(wave_ref[part], hot_y).astype(bf16)
        t_ref[part, :, :STICKS] = table
        t_ref[part, :128, STICKS:] = -table[128:]
        t_ref[part, 128:, STICKS:] = table[:128]
    v_ref[...] = jnp.zeros_like(v_ref)

    def lay_out(g, carry):
        block = potential_ref[:, pl.ds(pl.multiple_of(896 * g, 128), 896)]
        for k in range(8):
            v_ref[8 * g + k, :PLANES, :GRID] = block[:, GRID * k : GRID * k + GRID]
        return carry

    lax.fori_loop(0, 14, lay_out, 0)

    freq_x, freq_y = frequency(index_x), frequency(index_y)
    lateral = freq_x * freq_x + freq_y * freq_y
    stick = lax.broadcasted_iota(jnp.int32, (OWN, STICKS), 1)
    mine = stick == lax.broadcasted_iota(jnp.int32, (OWN, STICKS), 0) + OWN * pencil
    own_lateral = jnp.sum(jnp.where(mine, lateral, 0.0), axis=1, keepdims=True)
    lane = lax.broadcasted_iota(jnp.int32, (OWN, 256), 1)
    freq_z = frequency(jnp.where(lane < 128, lane, lane - 128))
    kinetic = 0.5 * (own_lateral + freq_z * freq_z) / float(RADIUS * RADIUS)

    each(lambda d: to_b(pencil_peer(d), pencil_peer(d)).wait_recv())
    got = recv_b[...].reshape(4, 16, 128)
    group = lax.div(lax.broadcasted_iota(jnp.int32, (16, 128), 1), 32)
    for q in range(4):
        out = got[0] if q == 0 else pltpu.roll(got[0], (-32 * q) % 128, 1)
        for p in range(1, 4):
            moved = got[p] if p == q else pltpu.roll(got[p], (32 * (p - q)) % 128, 1)
            out = jnp.where(group == p, moved, out)
        for t in range(4):
            psi_ref[q // 2, 4 * (q % 2) : 4 * (q % 2) + 4, 128 * t : 128 * t + 128] = out[4 * t : 4 * t + 4]

    psi_r, psi_i = psi_ref[0], psi_ref[1]

    def phases(x):
        return a_ref[pl.ds(x, 1), :], a_ref[pl.ds(128 + x, 1), :]

    def spread(n, carry):
        real, imag = [], []
        for k in range(2):
            a_r, a_i = phases(2 * n + k)
            real.append(a_r * psi_r - a_i * psi_i)
            imag.append(a_r * psi_i + a_i * psi_r)
        rows = pl.ds(pl.multiple_of(16 * n, 16), 16)
        p_ref[0, rows, :STICKS], p_ref[1, rows, :STICKS] = split(jnp.concatenate(real, axis=0))
        p_ref[0, rows, STICKS:], p_ref[1, rows, STICKS:] = split(jnp.concatenate(imag, axis=0))
        return carry

    lax.fori_loop(0, 56, spread, 0)

    u = dot3((p_ref[0], p_ref[1]), (t_ref[0], t_ref[1]), NT)
    v = v_ref[...].reshape(896, 128)
    for part in range(2):
        cols = slice(128 * part, 128 * part + 128)
        w_ref[0, :, cols], w_ref[1, :, cols] = split(u[:, cols] * v)

    def back_rows(n, carry):
        rows = pl.ds(pl.multiple_of(448 * n, 448), 448)
        c_ref[rows, :] = dot3((w_ref[0, rows, :], w_ref[1, rows, :]), (t_ref[0], t_ref[1]))
        return carry

    lax.fori_loop(0, 2, back_rows, 0)

    def collect(n, carry):
        w_r, w_i = carry
        for k in range(4):
            x = 4 * n + k
            a_r, a_i = phases(x)
            rows = pl.ds(pl.multiple_of(8 * x, 8), 8)
            c_r, c_i = c_ref[rows, :STICKS], c_ref[rows, STICKS:]
            w_r = w_r + (a_r * c_r + a_i * c_i)
            w_i = w_i + (a_r * c_i - a_i * c_r)
        return w_r, w_i

    zero = jnp.zeros((8, STICKS), f32)
    sums = lax.fori_loop(0, 28, collect, (zero, zero))

    outs = []
    for q in range(4):
        half = sums[q // 2][4 * (q % 2) : 4 * (q % 2) + 4]
        outs.append(jnp.concatenate([half[:, 128 * t : 128 * t + 128] for t in range(4)], axis=0))
    for p in range(4):
        out = outs[0] if p == 0 else pltpu.roll(outs[0], (-32 * p) % 128, 1)
        for q in range(1, 4):
            moved = outs[q] if p == q else pltpu.roll(outs[q], (32 * (q - p)) % 128, 1)
            out = jnp.where(group == q, moved, out)
        send_d[4 * p : 4 * p + 4] = out.reshape(4, 4, 128)
    each(lambda d: to_d(pencil_peer(d), pencil).start())
    recv_d[pencil] = send_d[slot_of(pencil)]

    pick = lax.broadcasted_iota(jnp.int32, (256, 128), 0)
    ones = jnp.ones((8, 256), f32)

    def gram_row(values, first):
        other = turned(values)

        def one(i, carry):
            member = bands_ref[i]
            real, imag = member * values, member * other
            rows = pl.ds(pl.multiple_of(8 * i, 8), 8)
            later = pl.ds(pl.multiple_of(128 + 8 * i, 8), 8)
            sums_ref[rows, :] = (real[:8] + real[8:16]) + (real[16:24] + real[24:])
            sums_ref[later, :] = (imag[:8] + imag[8:16]) + (imag[16:24] + imag[24:])
            return carry

        lax.fori_loop(0, BANDS, one, 0)
        target = lax.broadcasted_iota(jnp.int32, (256, 128), 1)
        chosen = jnp.where(lax.div(pick, 8) + first == target, 1.0, 0.0)
        return dot_exact(dot_exact(ones, sums_ref[...], NT), chosen)[:1]

    def hand_on_p(d):
        to_p(chip_peer(d), chip_peer(d)).wait_recv()
        hand_p(chip_peer(d)).start()

    chips(hand_on_p)
    chips(lambda d: hand_p(lax.rem(sibling + 2 * d, BANDS)).wait_recv(), 0)
    overlap_row = gram_row(own, 32)

    each(lambda d: to_d(pencil_peer(d), pencil_peer(d)).wait_recv())
    back = split(recv_d[...].reshape(64, 128).T)
    own_h = kinetic * own
    for q in range(4):
        rows, cols = slice(32 * q, 32 * q + 32), slice(256 * q, 256 * q + 256)
        own_h = own_h + dot3(
            (back[0][rows], back[1][rows]), (forward_ref[0, :, cols], forward_ref[1, :, cols])
        )
    bands_h_ref[band] = own_h
    chips(lambda d: to_h(chip_peer(d), band).start())
    hand_h(band).start()

    send_g[...] = gram_row(own_h, 0) + overlap_row
    each(lambda d: to_g(pencil_peer(d), pencil).start())
    recv_g[pencil] = send_g[...]
    each(lambda d: to_g(pencil_peer(d), pencil_peer(d)).wait_recv())
    row_ref[...] = jnp.sum(recv_g[...], axis=0) / float(STICKS * GRID)
    each(lambda d: to_r(band_peer(d), band).start())
    recv_r[band] = row_ref[...]
    for d in (1, 7, 2, 6, 3, 5, 4):
        to_h(chip_peer(d), chip_peer(d)).wait_recv()
        hand_h(chip_peer(d)).start()

    x_r, x_i = ritz_ref[0], ritz_ref[1]
    xt = jnp.concatenate([x_r.T, x_i.T], axis=1)
    conj = jnp.concatenate(
        [jnp.concatenate([x_r, -x_i], axis=1), jnp.concatenate([x_i, x_r], axis=1)], axis=0
    )
    each(lambda d: to_r(band_peer(d), band_peer(d)).wait_recv())
    grams = recv_r[...].reshape(BANDS, 128)
    lane = lax.broadcasted_iota(jnp.int32, (BANDS, 128), 1)
    swapped = jnp.where(lax.rem(lane, 32) < 16, -pltpu.roll(grams, 112, 1), pltpu.roll(grams, 16, 1))
    half = dot_exact(xt, jnp.concatenate([grams, swapped], axis=0))
    energy = dot_exact(half[:, :32], conj)
    metric = dot_exact(half[:, 32:64], conj)
    row16 = lax.broadcasted_iota(jnp.int32, (BANDS, 16), 0)
    diagonal = row16 == lax.broadcasted_iota(jnp.int32, (BANDS, 16), 1)
    ratio = jnp.where(diagonal, energy[:, :16] / metric[:, :16], 0.0)
    value_j = jnp.sum(ratio, axis=1, keepdims=True)
    value_i = jnp.sum(ratio, axis=0, keepdims=True)
    values_ref[...] = value_i
    spacing = value_j - value_i
    factor = spacing / jnp.maximum(spacing * spacing, (0.25 / BANDS) ** 2)
    residual_r = jnp.where(diagonal, 1.0, 0.0) - metric[:, :16]
    residual_i = -metric[:, 16:]
    update_r = jnp.where(diagonal, 0.5 * residual_r, (energy[:, :16] + value_j * residual_r) * factor)
    update_i = jnp.where(diagonal, 0.5 * residual_i, (energy[:, 16:] + value_j * residual_i) * factor)
    chosen = row16 == band
    u_r = jnp.sum(jnp.where(chosen, update_r + jnp.where(diagonal, 1.0, 0.0), 0.0), axis=0, keepdims=True)
    u_i = jnp.sum(jnp.where(chosen, update_i, 0.0), axis=0, keepdims=True)
    new_r = jnp.sum(x_r * u_r - x_i * u_i, axis=1, keepdims=True)
    new_i = jnp.sum(x_r * u_i + x_i * u_r, axis=1, keepdims=True)

    def rotate(members):
        along = jnp.zeros((OWN, 256), f32)
        across = jnp.zeros((OWN, 256), f32)
        for i in range(BANDS):
            member = members[i]
            along = along + new_r[i : i + 1] * member
            across = across + new_i[i : i + 1] * member
        return narrow(along - turned(across))[:, : 2 * GRID]

    refined_ref[0] = rotate(bands_ref)
    chips(lambda d: hand_h(lax.rem(sibling + 2 * d, BANDS)).wait_recv(), 0)
    refined_h_ref[0] = rotate(bands_h_ref)

    def finish(d):
        to_b(pencil_peer(d), pencil).wait_send()
        to_d(pencil_peer(d), pencil).wait_send()
        to_g(pencil_peer(d), pencil).wait_send()
        to_r(band_peer(d), band).wait_send()

    each(finish)
    chips(lambda d: to_p(chip_peer(d), band).wait_send())
    chips(lambda d: to_h(chip_peer(d), band).wait_send())
    chips(lambda d: hand_p(chip_peer(d)).wait_send(), 0)
    chips(lambda d: hand_h(chip_peer(d)).wait_send(), 0)


def emit(*refs):
    for k in range(3):
        refs[3 + k][...] = refs[k][...]


def shards(coeffs, columns, potential, ritz_vectors):
    inverse, forward = z_tables()
    vmem = pl.BlockSpec(memory_space=pltpu.VMEM)
    outs = (
        jax.ShapeDtypeStruct((1, OWN, 2 * GRID), f32),
        jax.ShapeDtypeStruct((1, OWN, 2 * GRID), f32),
        jax.ShapeDtypeStruct((1, BANDS), f32),
    )
    results = pl.pallas_call(
        kernel,
        out_shape=tuple(pltpu.VMEM(o.shape, f32) for o in outs),
        in_specs=[pl.BlockSpec(memory_space=pltpu.HBM)] * 7,
        out_specs=(vmem,) * 3,
        scratch_shapes=[
            pltpu.VMEM((1, OWN, 2 * GRID), f32),
            pltpu.VMEM((1, STICKS), jnp.int32),
            pltpu.VMEM((PLANES, GRID * GRID), f32),
            pltpu.VMEM((2, BANDS, BANDS), f32),
            pltpu.VMEM((2, 64, 1024), bf16),
            pltpu.VMEM((2, 64, 1024), bf16),
            pltpu.VMEM((3, 256, 128), bf16),
            pltpu.SemaphoreType.DMA((7,)),
            pltpu.VMEM((OWN, 256), f32),
            pltpu.VMEM((2, 128, 1024), bf16),
            pltpu.VMEM((16, 4, 128), f32),
            pltpu.VMEM((16, 4, 128), f32),
            pltpu.VMEM((16, 4, 128), f32),
            pltpu.VMEM((16, 4, 128), f32),
            pltpu.VMEM((2, 8, STICKS), f32),
            pltpu.VMEM((256, STICKS), f32),
            pltpu.VMEM((2, 256, 1024), bf16),
            pltpu.VMEM((GRID, 8, 128), f32),
            pltpu.VMEM((2, 896, 1024), bf16),
            pltpu.VMEM((2, 896, 256), bf16),
            pltpu.VMEM((896, 1024), f32),
            pltpu.VMEM((BANDS, OWN, 256), f32),
            pltpu.VMEM((BANDS, OWN, 256), f32),
            pltpu.VMEM((256, 256), f32),
            pltpu.VMEM((1, 128), f32),
            pltpu.VMEM((16, 1, 128), f32),
            pltpu.VMEM((1, 128), f32),
            pltpu.VMEM((16, 1, 128), f32),
        ]
        + [pltpu.SemaphoreType.DMA((16,))] * 14,
        compiler_params=pltpu.CompilerParams(
            collective_id=0, has_side_effects=True, vmem_limit_bytes=62 * 2**20
        ),
    )(
        coeffs,
        columns.reshape(1, STICKS),
        potential,
        ritz_vectors,
        jnp.asarray(inverse),
        jnp.asarray(forward),
        jnp.asarray(wave_table()),
    )
    anywhere = pl.BlockSpec(memory_space=pl.ANY)
    refined, refined_h, values = pl.pallas_call(
        emit,
        out_shape=outs,
        in_specs=[vmem] * 3,
        out_specs=(vmem,) * 3,
        compiler_params=pltpu.CompilerParams(vmem_limit_bytes=2**20),
    )(*results)
    return refined, refined_h, values.reshape(BANDS)


def solution(mesh):
    return jax.shard_map(
        shards,
        mesh=mesh,
        in_specs=(P("band", "pencil", None), P(), P("pencil", None), P()),
        out_specs=(P("band", "pencil", None), P("band", "pencil", None), P()),
        check_vma=False,
    )
```

```python
import functools

import jax
import jax.numpy as jnp
import ml_dtypes
import numpy as np
from jax import lax
from jax.experimental import pallas as pl
from jax.experimental.pallas import tpu as pltpu
from jax.sharding import PartitionSpec as P

GRID = 112
BANDS = 16
PENCILS = 16
PLANES = 7
STICKS = 512
OWN = 32
RADIUS = 28
NEAR = (1, 7, 2, 6, 3, 5, 4)

f32 = jnp.float32
bf16 = jnp.bfloat16
MESH = pl.DeviceIdType.MESH
NN = (((1,), (0,)), ((), ()))
NT = (((1,), (1,)), ((), ()))


def parts_of(table, count):
    parts = []
    for _ in range(count):
        part = table.astype(ml_dtypes.bfloat16)
        parts.append(part)
        table = table - part.astype(np.float64)
    return np.stack(parts)


def wave_table():
    index = np.arange(GRID)
    angle = 2.0 * np.pi * (np.outer(index, index) % GRID) / GRID
    table = np.zeros((256, 128))
    table[:GRID, :GRID] = np.cos(angle)
    table[128 : 128 + GRID, :GRID] = np.sin(angle)
    return parts_of(table, 3)


def z_tables():
    table = np.zeros((4, PENCILS, 4, 256))
    k = np.arange(GRID)
    for p in range(PENCILS):
        for r in range(4):
            for q in range(4):
                z = 4 * (q % 2) + r
                if z >= PLANES:
                    continue
                angle = 2.0 * np.pi * ((k * (PLANES * p + z)) % GRID) / GRID
                cosine, sine = np.cos(angle), np.sin(angle)
                real = q // 2 == 0
                table[q, p, r, :GRID] = cosine if real else sine
                table[q, p, r, 128 : 128 + GRID] = -sine if real else cosine
    table = table.reshape(256, 256)
    return parts_of(table, 2), parts_of(table / float(GRID) ** 3, 2)


def split(x):
    high = x.astype(bf16)
    return high, (x - high.astype(f32)).astype(bf16)


def dot(a, b, dims=NN):
    return lax.dot_general(a, b, dims, preferred_element_type=f32)


def dot3(a, b, dims=NN):
    return dot(a[0], b[0], dims) + dot(a[0], b[1], dims) + dot(a[1], b[0], dims)


def dot_exact(a, b, dims=NN):
    return lax.dot_general(a, b, dims, precision=lax.Precision.HIGHEST, preferred_element_type=f32)


def slot_of(p):
    return lax.rem(p, 4) * 4 + lax.div(p, 4)


def frequency(index):
    return jnp.where(index < GRID // 2, index, index - GRID).astype(f32)


def wide(x):
    lane = lax.broadcasted_iota(jnp.int32, x.shape, 1)
    moved = pltpu.roll(x, 16, 1)
    return jnp.where(lane < GRID, x, jnp.where(lane < 128, 0.0, moved))


def narrow(x):
    lane = lax.broadcasted_iota(jnp.int32, x.shape, 1)
    moved = pltpu.roll(x, 240, 1)
    return jnp.where(lane < GRID, x, moved)


def turned(x):
    return jnp.concatenate([x[:, 128:], -x[:, :128]], axis=1)


def kernel(
    coeffs_hbm, columns_hbm, potential_hbm, ritz_hbm, inverse_hbm, forward_hbm, wave_hbm,
    refined_ref, refined_h_ref, values_ref,
    coeffs_ref, columns_ref, potential_ref, ritz_ref, inverse_ref, forward_ref, wave_ref, sem_in,
    pad_ref, rows_ref, scale_ref, send_b, recv_b, send_d, recv_d, psi_ref, a_ref, t_ref, v_ref, p_ref, w_ref, c_ref,
    bands_ref, bands_h_ref, sums_ref, send_g, recv_g, row_ref, recv_r,
    sem_sb, sem_rb, sem_sd, sem_rd, sem_sp, sem_fp, sem_rp, sem_sh, sem_fh, sem_rh, sem_sg, sem_rg, sem_sr, sem_rr,
):
    pencil = lax.axis_index("pencil")
    band = lax.axis_index("band")

    def pencil_peer(d):
        return lax.rem(pencil + d, PENCILS)

    def band_peer(d):
        return lax.rem(band + d, BANDS)

    def each(body):
        for d in range(1, 16):
            body(d)

    def to_b(p, mine):
        return pltpu.make_async_remote_copy(
            send_b.at[p], recv_b.at[slot_of(mine)], sem_sb.at[p], sem_rb.at[mine],
            device_id=(p, band), device_id_type=MESH,
        )

    def to_d(p, mine):
        return pltpu.make_async_remote_copy(
            send_d.at[slot_of(p)], recv_d.at[mine], sem_sd.at[p], sem_rd.at[mine],
            device_id=(p, band), device_id_type=MESH,
        )

    def to_g(p, mine):
        return pltpu.make_async_remote_copy(
            send_g, recv_g.at[mine], sem_sg.at[p], sem_rg.at[mine], device_id=(p, band), device_id_type=MESH
        )

    sibling = band + 1 - 2 * lax.rem(band, 2)

    def chip_peer(d):
        return lax.rem(band + 2 * d, BANDS)

    def to_p(b, mine):
        return pltpu.make_async_remote_copy(
            bands_ref.at[mine], bands_ref.at[mine], sem_sp.at[b], sem_rp.at[mine],
            device_id=(pencil, b), device_id_type=MESH,
        )

    def hand_p(q):
        return pltpu.make_async_remote_copy(
            bands_ref.at[q], bands_ref.at[q], sem_fp.at[q], sem_rp.at[q],
            device_id=(pencil, sibling), device_id_type=MESH,
        )

    def to_h(b, mine):
        return pltpu.make_async_remote_copy(
            bands_h_ref.at[mine], bands_h_ref.at[mine], sem_sh.at[b], sem_rh.at[mine],
            device_id=(pencil, b), device_id_type=MESH,
        )

    def hand_h(q):
        return pltpu.make_async_remote_copy(
            bands_h_ref.at[q], bands_h_ref.at[q], sem_fh.at[q], sem_rh.at[q],
            device_id=(pencil, sibling), device_id_type=MESH,
        )

    def chips(body, first=1):
        def step(d, carry):
            body(d)
            return carry

        lax.fori_loop(first, 8, step, 0)

    def to_r(b, mine):
        return pltpu.make_async_remote_copy(
            row_ref, recv_r.at[mine], sem_sr.at[b], sem_rr.at[mine], device_id=(pencil, b), device_id_type=MESH
        )

    sources = (coeffs_hbm, inverse_hbm, columns_hbm, wave_hbm, potential_hbm, forward_hbm, ritz_hbm)
    targets = (coeffs_ref, inverse_ref, columns_ref, wave_ref, potential_ref, forward_ref, ritz_ref)
    loads = [pltpu.make_async_copy(a, b, sem_in.at[k]) for k, (a, b) in enumerate(zip(sources, targets))]
    barrier = pltpu.get_barrier_semaphore()
    for load in loads[:2]:
        load.start()

    def greet(d):
        pl.semaphore_signal(barrier, inc=1, device_id=(pencil_peer(d), band), device_id_type=MESH)
        pl.semaphore_signal(barrier, inc=1, device_id=(pencil, band_peer(d)), device_id_type=MESH)

    each(greet)
    for load in loads[2:]:
        load.start()
    pad_ref[...] = jnp.zeros_like(pad_ref)
    rows_ref[...] = jnp.zeros_like(rows_ref)
    for load in loads[:2]:
        load.wait()

    pad_ref[:, : 2 * GRID] = coeffs_ref[0]
    own = wide(pad_ref[...])
    bands_ref[band] = own
    group = lax.div(lax.broadcasted_iota(jnp.int32, (64, 128), 1), 32)
    copies = jnp.concatenate([own] * 4, axis=0)
    planes = dot3((inverse_ref[0], inverse_ref[1]), split(copies), NT)
    packed = planes[:64]
    for q in range(1, 4):
        packed = jnp.where(group == q, planes[64 * q : 64 * q + 64], packed)
    send_b[...] = packed.reshape(PENCILS, 4, 128)

    pl.semaphore_wait(barrier, 30)
    each(lambda d: to_b(pencil_peer(d), pencil).start())
    chips(lambda d: to_p(chip_peer(d), band).start())
    hand_p(band).start()
    recv_b[slot_of(pencil)] = send_b[pencil]
    for load in loads[2:]:
        load.wait()

    columns = columns_ref[...]
    index_x = lax.div(columns, GRID)
    index_y = lax.rem(columns, GRID)
    row = lax.broadcasted_iota(jnp.int32, (128, STICKS), 0)
    hot_x = jnp.where(row == index_x, 1.0, 0.0).astype(bf16)
    hot_y = jnp.where(row == index_y, 1.0, 0.0).astype(bf16)
    a_ref[...] = dot(wave_ref[0], hot_x) + dot(wave_ref[1], hot_x) + dot(wave_ref[2], hot_x)
    for part in range(2):
        table = dot(wave_ref[part], hot_y).astype(bf16)
        t_ref[part, :, :STICKS] = table
        t_ref[part, :128, STICKS:] = -table[128:]
        t_ref[part, 128:, STICKS:] = table[:128]
    v_ref[...] = jnp.zeros_like(v_ref)

    def lay_out(g, carry):
        block = potential_ref[:, pl.ds(pl.multiple_of(896 * g, 128), 896)]
        for k in range(8):
            v_ref[8 * g + k, :PLANES, :GRID] = block[:, GRID * k : GRID * k + GRID]
        return carry

    lax.fori_loop(0, 14, lay_out, 0)

    freq_x, freq_y = frequency(index_x), frequency(index_y)
    lateral = freq_x * freq_x + freq_y * freq_y
    stick = lax.broadcasted_iota(jnp.int32, (OWN, STICKS), 1)
    mine = stick == lax.broadcasted_iota(jnp.int32, (OWN, STICKS), 0) + OWN * pencil
    own_lateral = jnp.sum(jnp.where(mine, lateral, 0.0), axis=1, keepdims=True)
    lane = lax.broadcasted_iota(jnp.int32, (OWN, 256), 1)
    freq_z = frequency(jnp.where(lane < 128, lane, lane - 128))
    kinetic = 0.5 * (own_lateral + freq_z * freq_z) / float(RADIUS * RADIUS)

    each(lambda d: to_b(pencil_peer(d), pencil_peer(d)).wait_recv())
    got = recv_b[...].reshape(4, 16, 128)
    group = group[:16]
    for q in range(4):
        out = got[0] if q == 0 else pltpu.roll(got[0], (-32 * q) % 128, 1)
        for p in range(1, 4):
            moved = got[p] if p == q else pltpu.roll(got[p], (32 * (p - q)) % 128, 1)
            out = jnp.where(group == p, moved, out)
        for t in range(4):
            psi_ref[q // 2, 4 * (q % 2) : 4 * (q % 2) + 4, 128 * t : 128 * t + 128] = out[4 * t : 4 * t + 4]

    psi_r, psi_i = psi_ref[0], psi_ref[1]

    def phases(x):
        return a_ref[pl.ds(x, 1), :], a_ref[pl.ds(128 + x, 1), :]

    def spread(n, carry):
        real, imag = [], []
        for k in range(2):
            a_r, a_i = phases(2 * n + k)
            real.append(a_r * psi_r - a_i * psi_i)
            imag.append(a_r * psi_i + a_i * psi_r)
        rows = pl.ds(pl.multiple_of(16 * n, 16), 16)
        p_ref[0, rows, :STICKS], p_ref[1, rows, :STICKS] = split(jnp.concatenate(real, axis=0))
        p_ref[0, rows, STICKS:], p_ref[1, rows, STICKS:] = split(jnp.concatenate(imag, axis=0))
        return carry

    lax.fori_loop(0, 56, spread, 0)

    u = dot3((p_ref[0], p_ref[1]), (t_ref[0], t_ref[1]), NT)
    v = v_ref[...].reshape(896, 128)
    for part in range(2):
        cols = slice(128 * part, 128 * part + 128)
        w_ref[0, :, cols], w_ref[1, :, cols] = split(u[:, cols] * v)

    def back_rows(n, carry):
        rows = pl.ds(pl.multiple_of(448 * n, 448), 448)
        c_ref[rows, :] = dot3((w_ref[0, rows, :], w_ref[1, rows, :]), (t_ref[0], t_ref[1]))
        return carry

    lax.fori_loop(0, 2, back_rows, 0)

    def collect(n, carry):
        w_r, w_i = carry
        for k in range(4):
            x = 4 * n + k
            a_r, a_i = phases(x)
            rows = pl.ds(pl.multiple_of(8 * x, 8), 8)
            c_r, c_i = c_ref[rows, :STICKS], c_ref[rows, STICKS:]
            w_r = w_r + (a_r * c_r + a_i * c_i)
            w_i = w_i + (a_r * c_i - a_i * c_r)
        return w_r, w_i

    zero = jnp.zeros((8, STICKS), f32)
    sums = lax.fori_loop(0, 28, collect, (zero, zero))

    outs = []
    for q in range(4):
        half = sums[q // 2][4 * (q % 2) : 4 * (q % 2) + 4]
        outs.append(jnp.concatenate([half[:, 128 * t : 128 * t + 128] for t in range(4)], axis=0))
    for p in range(4):
        out = outs[0] if p == 0 else pltpu.roll(outs[0], (-32 * p) % 128, 1)
        for q in range(1, 4):
            moved = outs[q] if p == q else pltpu.roll(outs[q], (32 * (q - p)) % 128, 1)
            out = jnp.where(group == q, moved, out)
        send_d[4 * p : 4 * p + 4] = out.reshape(4, 4, 128)
    each(lambda d: to_d(pencil_peer(d), pencil).start())
    recv_d[pencil] = send_d[slot_of(pencil)]

    def gram_rows(values, first):
        other = turned(values)

        def one(n, carry):
            for k in range(4):
                i = 4 * n + k
                member = bands_ref[i]
                for part, factor in enumerate((values, other)):
                    products = member * factor
                    folded = (products[:8] + products[8:16]) + (products[16:24] + products[24:])
                    rows = pl.ds(pl.multiple_of(128 * part + 8 * i, 8), 8)
                    sums_ref[rows, :] = folded[:, :128] + folded[:, 128:]
            return carry

        lax.fori_loop(0, 4, one, 0)
        rows_ref[first : first + 32, :] = jnp.sum(sums_ref[...].reshape(32, 8, 128), axis=1)

    def hand_on_p(d):
        to_p(chip_peer(d), chip_peer(d)).wait_recv()
        hand_p(chip_peer(d)).start()

    chips(hand_on_p)
    chips(lambda d: hand_p(lax.rem(sibling + 2 * d, BANDS)).wait_recv(), 0)
    gram_rows(own, 32)

    each(lambda d: to_d(pencil_peer(d), pencil_peer(d)).wait_recv())
    arrived = recv_d[...].reshape(64, 128)
    back = jnp.concatenate([arrived, arrived], axis=0).T
    low_half = lax.broadcasted_iota(jnp.int32, (OWN, 128), 1) < 64
    lined = jnp.concatenate(
        [jnp.where(low_half, back[64 * h : 64 * h + 32], back[64 * h + 32 : 64 * h + 64]) for h in range(2)], axis=1
    )
    own_h = kinetic * own + dot3(split(lined), (forward_ref[0], forward_ref[1]))
    bands_h_ref[band] = own_h
    for d in NEAR[::-1]:
        to_h(chip_peer(d), band).start()
    hand_h(band).start()

    gram_rows(own_h, 0)
    send_g[...] = dot_exact(jnp.ones((8, 128), f32), rows_ref[...], NT)[:1]
    each(lambda d: to_g(pencil_peer(d), pencil).start())
    recv_g[pencil] = send_g[...]
    each(lambda d: to_g(pencil_peer(d), pencil_peer(d)).wait_recv())
    row_ref[...] = jnp.sum(recv_g[...], axis=0) / float(STICKS * GRID)
    each(lambda d: to_r(band_peer(d), band).start())
    recv_r[band] = row_ref[...]
    for d in NEAR:
        to_h(chip_peer(d), chip_peer(d)).wait_recv()
        hand_h(chip_peer(d)).start()

    x_r, x_i = ritz_ref[0], ritz_ref[1]
    xt = jnp.concatenate([x_r.T, x_i.T], axis=1)
    conj = jnp.concatenate(
        [jnp.concatenate([x_r, -x_i], axis=1), jnp.concatenate([x_i, x_r], axis=1)], axis=0
    )
    each(lambda d: to_r(band_peer(d), band_peer(d)).wait_recv())
    grams = recv_r[...].reshape(BANDS, 128)
    lane = lax.broadcasted_iota(jnp.int32, (BANDS, 128), 1)
    swapped = jnp.where(lax.rem(lane, 32) < 16, -pltpu.roll(grams, 112, 1), pltpu.roll(grams, 16, 1))
    half = dot_exact(xt, jnp.concatenate([grams, swapped], axis=0))
    energy = dot_exact(half[:, :32], conj)
    metric = dot_exact(half[:, 32:64], conj)
    row16 = lax.broadcasted_iota(jnp.int32, (BANDS, 16), 0)
    diagonal = row16 == lax.broadcasted_iota(jnp.int32, (BANDS, 16), 1)
    ratio = jnp.where(diagonal, energy[:, :16] / metric[:, :16], 0.0)
    value_j = jnp.sum(ratio, axis=1, keepdims=True)
    value_i = jnp.sum(ratio, axis=0, keepdims=True)
    values_ref[...] = value_i
    spacing = value_j - value_i
    factor = spacing / jnp.maximum(spacing * spacing, (0.25 / BANDS) ** 2)
    residual_r = jnp.where(diagonal, 1.0, 0.0) - metric[:, :16]
    residual_i = -metric[:, 16:]
    update_r = jnp.where(diagonal, 0.5 * residual_r, (energy[:, :16] + value_j * residual_r) * factor)
    update_i = jnp.where(diagonal, 0.5 * residual_i, (energy[:, 16:] + value_j * residual_i) * factor)
    chosen = row16 == band
    u_r = jnp.sum(jnp.where(chosen, update_r + jnp.where(diagonal, 1.0, 0.0), 0.0), axis=0, keepdims=True)
    u_i = jnp.sum(jnp.where(chosen, update_i, 0.0), axis=0, keepdims=True)
    new_r = jnp.sum(x_r * u_r - x_i * u_i, axis=1, keepdims=True)
    new_i = jnp.sum(x_r * u_i + x_i * u_r, axis=1, keepdims=True)

    scale_ref[0] = jnp.broadcast_to(new_r, (BANDS, 256))
    scale_ref[1] = jnp.broadcast_to(new_i, (BANDS, 256))

    def add(sums, i, members):
        member = members[i]
        return sums[0] + scale_ref[0, pl.ds(i, 1), :] * member, sums[1] + scale_ref[1, pl.ds(i, 1), :] * member

    def rotated(sums):
        return narrow(sums[0] - turned(sums[1]))[:, : 2 * GRID]

    empty = (jnp.zeros((OWN, 256), f32),) * 2
    sums = empty
    for i in range(BANDS):
        sums = add(sums, i, bands_ref)
    refined_ref[0] = rotated(sums)
    sums = empty
    for d in range(8):
        sums = add(sums, chip_peer(d), bands_h_ref)
    for d in (0,) + NEAR:
        i = lax.rem(sibling + 2 * d, BANDS)
        hand_h(i).wait_recv()
        sums = add(sums, i, bands_h_ref)
    refined_h_ref[0] = rotated(sums)

    def finish(d):
        to_b(pencil_peer(d), pencil).wait_send()
        to_d(pencil_peer(d), pencil).wait_send()
        to_g(pencil_peer(d), pencil).wait_send()
        to_r(band_peer(d), band).wait_send()

    each(finish)
    chips(lambda d: to_p(chip_peer(d), band).wait_send())
    chips(lambda d: to_h(chip_peer(d), band).wait_send())
    chips(lambda d: hand_p(chip_peer(d)).wait_send(), 0)
    chips(lambda d: hand_h(chip_peer(d)).wait_send(), 0)


def emit(*refs):
    for k in range(3):
        refs[3 + k][...] = refs[k][...]


def shards(coeffs, columns, potential, ritz_vectors):
    inverse, forward = z_tables()
    vmem = pl.BlockSpec(memory_space=pltpu.VMEM)
    outs = (
        jax.ShapeDtypeStruct((1, OWN, 2 * GRID), f32),
        jax.ShapeDtypeStruct((1, OWN, 2 * GRID), f32),
        jax.ShapeDtypeStruct((1, BANDS), f32),
    )
    results = pl.pallas_call(
        kernel,
        out_shape=tuple(pltpu.VMEM(o.shape, f32) for o in outs),
        in_specs=[pl.BlockSpec(memory_space=pltpu.HBM)] * 7,
        out_specs=(vmem,) * 3,
        scratch_shapes=[
            pltpu.VMEM((1, OWN, 2 * GRID), f32),
            pltpu.VMEM((1, STICKS), jnp.int32),
            pltpu.VMEM((PLANES, GRID * GRID), f32),
            pltpu.VMEM((2, BANDS, BANDS), f32),
            pltpu.VMEM((2, 256, 256), bf16),
            pltpu.VMEM((2, 256, 256), bf16),
            pltpu.VMEM((3, 256, 128), bf16),
            pltpu.SemaphoreType.DMA((7,)),
            pltpu.VMEM((OWN, 256), f32),
            pltpu.VMEM((128, 128), f32),
            pltpu.VMEM((2, BANDS, 256), f32),
            pltpu.VMEM((16, 4, 128), f32),
            pltpu.VMEM((16, 4, 128), f32),
            pltpu.VMEM((16, 4, 128), f32),
            pltpu.VMEM((16, 4, 128), f32),
            pltpu.VMEM((2, 8, STICKS), f32),
            pltpu.VMEM((256, STICKS), f32),
            pltpu.VMEM((2, 256, 1024), bf16),
            pltpu.VMEM((GRID, 8, 128), f32),
            pltpu.VMEM((2, 896, 1024), bf16),
            pltpu.VMEM((2, 896, 256), bf16),
            pltpu.VMEM((896, 1024), f32),
            pltpu.VMEM((BANDS, OWN, 256), f32),
            pltpu.VMEM((BANDS, OWN, 256), f32),
            pltpu.VMEM((256, 128), f32),
            pltpu.VMEM((1, 128), f32),
            pltpu.VMEM((16, 1, 128), f32),
            pltpu.VMEM((1, 128), f32),
            pltpu.VMEM((16, 1, 128), f32),
        ]
        + [pltpu.SemaphoreType.DMA((16,))] * 14,
        compiler_params=pltpu.CompilerParams(
            collective_id=0, has_side_effects=True, vmem_limit_bytes=62 * 2**20
        ),
    )(
        coeffs,
        columns.reshape(1, STICKS),
        potential,
        ritz_vectors,
        jnp.asarray(inverse),
        jnp.asarray(forward),
        jnp.asarray(wave_table()),
    )
    anywhere = pl.BlockSpec(memory_space=pl.ANY)
    refined, refined_h, values = pl.pallas_call(
        emit,
        out_shape=outs,
        in_specs=[vmem] * 3,
        out_specs=(vmem,) * 3,
        compiler_params=pltpu.CompilerParams(vmem_limit_bytes=2**20),
    )(*results)
    return refined, refined_h, values.reshape(BANDS)


def solution(mesh):
    return jax.shard_map(
        shards,
        mesh=mesh,
        in_specs=(P("band", "pencil", None), P(), P("pencil", None), P()),
        out_specs=(P("band", "pencil", None), P("band", "pencil", None), P()),
        check_vma=False,
    )
```

```python
import functools

import jax
import jax.numpy as jnp
import ml_dtypes
import numpy as np
from jax import lax
from jax.experimental import pallas as pl
from jax.experimental.pallas import tpu as pltpu
from jax.sharding import PartitionSpec as P

GRID = 112
BANDS = 16
PENCILS = 16
PLANES = 7
STICKS = 512
OWN = 32
RADIUS = 28
NEAR = (1, 7, 2, 6, 3, 5, 4)


def hops(step, size):
    return min(step, size - step)


PENCIL_STEPS = sorted(
    [(dx, dy) for dx in range(4) for dy in range(4) if dx or dy], key=lambda d: -hops(d[0], 4) - hops(d[1], 4)
)
BAND_STEPS = sorted([(dz, other) for dz in range(8) for other in range(2) if dz or other], key=lambda d: -hops(d[0], 8))

f32 = jnp.float32
bf16 = jnp.bfloat16
MESH = pl.DeviceIdType.MESH
NN = (((1,), (0,)), ((), ()))
NT = (((1,), (1,)), ((), ()))


def parts_of(table, count):
    parts = []
    for _ in range(count):
        part = table.astype(ml_dtypes.bfloat16)
        parts.append(part)
        table = table - part.astype(np.float64)
    return np.stack(parts)


def wave_table():
    index = np.arange(GRID)
    angle = 2.0 * np.pi * (np.outer(index, index) % GRID) / GRID
    table = np.zeros((256, 128))
    table[:GRID, :GRID] = np.cos(angle)
    table[128 : 128 + GRID, :GRID] = np.sin(angle)
    return parts_of(table, 3)


def z_tables():
    table = np.zeros((4, PENCILS, 4, 256))
    k = np.arange(GRID)
    for p in range(PENCILS):
        for r in range(4):
            for q in range(4):
                z = 4 * (q % 2) + r
                if z >= PLANES:
                    continue
                angle = 2.0 * np.pi * ((k * (PLANES * p + z)) % GRID) / GRID
                cosine, sine = np.cos(angle), np.sin(angle)
                real = q // 2 == 0
                table[q, p, r, :GRID] = cosine if real else sine
                table[q, p, r, 128 : 128 + GRID] = -sine if real else cosine
    table = table.reshape(256, 256)
    return parts_of(table, 2), parts_of(table / float(GRID) ** 3, 2)


def split(x):
    high = x.astype(bf16)
    return high, (x - high.astype(f32)).astype(bf16)


def dot(a, b, dims=NN):
    return lax.dot_general(a, b, dims, preferred_element_type=f32)


def dot3(a, b, dims=NN):
    return dot(a[0], b[0], dims) + dot(a[0], b[1], dims) + dot(a[1], b[0], dims)


def dot_exact(a, b, dims=NN):
    return lax.dot_general(a, b, dims, precision=lax.Precision.HIGHEST, preferred_element_type=f32)


def slot_of(p):
    return lax.rem(p, 4) * 4 + lax.div(p, 4)


def frequency(index):
    return jnp.where(index < GRID // 2, index, index - GRID).astype(f32)


def wide(x):
    lane = lax.broadcasted_iota(jnp.int32, x.shape, 1)
    moved = pltpu.roll(x, 16, 1)
    return jnp.where(lane < GRID, x, jnp.where(lane < 128, 0.0, moved))


def narrow(x):
    lane = lax.broadcasted_iota(jnp.int32, x.shape, 1)
    moved = pltpu.roll(x, 240, 1)
    return jnp.where(lane < GRID, x, moved)


def turned(x):
    return jnp.concatenate([x[:, 128:], -x[:, :128]], axis=1)


def kernel(
    coeffs_hbm, columns_hbm, potential_hbm, ritz_hbm, inverse_hbm, forward_hbm, wave_hbm,
    refined_ref, refined_h_ref, values_ref,
    coeffs_ref, columns_ref, potential_ref, ritz_ref, inverse_ref, forward_ref, wave_ref, sem_in,
    pad_ref, rows_ref, scale_ref, send_b, recv_b, send_d, recv_d, psi_ref, a_ref, t_ref, v_ref, p_ref, w_ref, c_ref,
    bands_ref, bands_h_ref, sums_ref, send_g, recv_g, row_ref, recv_r,
    sem_sb, sem_rb, sem_sd, sem_rd, sem_sp, sem_fp, sem_rp, sem_sh, sem_fh, sem_rh, sem_sg, sem_rg, sem_sr, sem_rr,
):
    pencil = lax.axis_index("pencil")
    band = lax.axis_index("band")

    x_own, y_own = lax.div(pencil, 4), lax.rem(pencil, 4)

    def pencil_peer(d):
        dx, dy = PENCIL_STEPS[d - 1]
        return 4 * lax.rem(x_own + dx, 4) + lax.rem(y_own + dy, 4)

    def band_peer(d):
        dz, other = BAND_STEPS[d - 1]
        core = lax.rem(band, 2)
        return lax.rem(2 * (lax.div(band, 2) + dz), BANDS) + (1 - core if other else core)

    def each(body):
        for d in range(1, 16):
            body(d)

    def to_b(p, mine):
        return pltpu.make_async_remote_copy(
            send_b.at[p], recv_b.at[slot_of(mine)], sem_sb.at[p], sem_rb.at[mine],
            device_id=(p, band), device_id_type=MESH,
        )

    def to_d(p, mine):
        return pltpu.make_async_remote_copy(
            send_d.at[slot_of(p)], recv_d.at[mine], sem_sd.at[p], sem_rd.at[mine],
            device_id=(p, band), device_id_type=MESH,
        )

    def to_g(p, mine):
        return pltpu.make_async_remote_copy(
            send_g, recv_g.at[mine], sem_sg.at[p], sem_rg.at[mine], device_id=(p, band), device_id_type=MESH
        )

    sibling = band + 1 - 2 * lax.rem(band, 2)

    def chip_peer(d):
        return lax.rem(band + 2 * d, BANDS)

    def to_p(b, mine):
        return pltpu.make_async_remote_copy(
            bands_ref.at[mine], bands_ref.at[mine], sem_sp.at[b], sem_rp.at[mine],
            device_id=(pencil, b), device_id_type=MESH,
        )

    def hand_p(q):
        return pltpu.make_async_remote_copy(
            bands_ref.at[q], bands_ref.at[q], sem_fp.at[q], sem_rp.at[q],
            device_id=(pencil, sibling), device_id_type=MESH,
        )

    def to_h(b, mine):
        return pltpu.make_async_remote_copy(
            bands_h_ref.at[mine], bands_h_ref.at[mine], sem_sh.at[b], sem_rh.at[mine],
            device_id=(pencil, b), device_id_type=MESH,
        )

    def hand_h(q):
        return pltpu.make_async_remote_copy(
            bands_h_ref.at[q], bands_h_ref.at[q], sem_fh.at[q], sem_rh.at[q],
            device_id=(pencil, sibling), device_id_type=MESH,
        )

    def chips(body, first=1):
        def step(d, carry):
            body(d)
            return carry

        lax.fori_loop(first, 8, step, 0)

    def to_r(b, mine):
        return pltpu.make_async_remote_copy(
            row_ref, recv_r.at[mine], sem_sr.at[b], sem_rr.at[mine], device_id=(pencil, b), device_id_type=MESH
        )

    sources = (coeffs_hbm, inverse_hbm, columns_hbm, wave_hbm, potential_hbm, forward_hbm, ritz_hbm)
    targets = (coeffs_ref, inverse_ref, columns_ref, wave_ref, potential_ref, forward_ref, ritz_ref)
    loads = [pltpu.make_async_copy(a, b, sem_in.at[k]) for k, (a, b) in enumerate(zip(sources, targets))]
    barrier = pltpu.get_barrier_semaphore()
    for load in loads[:2]:
        load.start()

    def greet(d):
        pl.semaphore_signal(barrier, inc=1, device_id=(pencil_peer(d), band), device_id_type=MESH)
        pl.semaphore_signal(barrier, inc=1, device_id=(pencil, band_peer(d)), device_id_type=MESH)

    each(greet)
    for load in loads[2:]:
        load.start()
    pad_ref[...] = jnp.zeros_like(pad_ref)
    rows_ref[...] = jnp.zeros_like(rows_ref)
    for load in loads[:2]:
        load.wait()

    pad_ref[:, : 2 * GRID] = coeffs_ref[0]
    own = wide(pad_ref[...])
    bands_ref[band] = own
    group = lax.div(lax.broadcasted_iota(jnp.int32, (64, 128), 1), 32)
    copies = jnp.concatenate([own] * 4, axis=0)
    planes = dot3((inverse_ref[0], inverse_ref[1]), split(copies), NT)
    packed = planes[:64]
    for q in range(1, 4):
        packed = jnp.where(group == q, planes[64 * q : 64 * q + 64], packed)
    send_b[...] = packed.reshape(PENCILS, 4, 128)

    pl.semaphore_wait(barrier, 30)
    each(lambda d: to_b(pencil_peer(d), pencil).start())
    chips(lambda d: to_p(chip_peer(d), band).start())
    hand_p(band).start()
    recv_b[slot_of(pencil)] = send_b[pencil]
    for load in loads[2:]:
        load.wait()

    columns = columns_ref[...]
    index_x = lax.div(columns, GRID)
    index_y = lax.rem(columns, GRID)
    row = lax.broadcasted_iota(jnp.int32, (128, STICKS), 0)
    hot_x = jnp.where(row == index_x, 1.0, 0.0).astype(bf16)
    hot_y = jnp.where(row == index_y, 1.0, 0.0).astype(bf16)
    a_ref[...] = dot(wave_ref[0], hot_x) + dot(wave_ref[1], hot_x) + dot(wave_ref[2], hot_x)
    for part in range(2):
        table = dot(wave_ref[part], hot_y).astype(bf16)
        t_ref[part, :, :STICKS] = table
        t_ref[part, :128, STICKS:] = -table[128:]
        t_ref[part, 128:, STICKS:] = table[:128]
    v_ref[...] = jnp.zeros_like(v_ref)

    def lay_out(g, carry):
        block = potential_ref[:, pl.ds(pl.multiple_of(896 * g, 128), 896)]
        for k in range(8):
            v_ref[8 * g + k, :PLANES, :GRID] = block[:, GRID * k : GRID * k + GRID]
        return carry

    lax.fori_loop(0, 14, lay_out, 0)

    freq_x, freq_y = frequency(index_x), frequency(index_y)
    lateral = freq_x * freq_x + freq_y * freq_y
    stick = lax.broadcasted_iota(jnp.int32, (OWN, STICKS), 1)
    mine = stick == lax.broadcasted_iota(jnp.int32, (OWN, STICKS), 0) + OWN * pencil
    own_lateral = jnp.sum(jnp.where(mine, lateral, 0.0), axis=1, keepdims=True)
    lane = lax.broadcasted_iota(jnp.int32, (OWN, 256), 1)
    freq_z = frequency(jnp.where(lane < 128, lane, lane - 128))
    kinetic = 0.5 * (own_lateral + freq_z * freq_z) / float(RADIUS * RADIUS)

    each(lambda d: to_b(pencil_peer(d), pencil_peer(d)).wait_recv())
    got = recv_b[...].reshape(4, 16, 128)
    group = group[:16]
    for q in range(4):
        out = got[0] if q == 0 else pltpu.roll(got[0], (-32 * q) % 128, 1)
        for p in range(1, 4):
            moved = got[p] if p == q else pltpu.roll(got[p], (32 * (p - q)) % 128, 1)
            out = jnp.where(group == p, moved, out)
        for t in range(4):
            psi_ref[q // 2, 4 * (q % 2) : 4 * (q % 2) + 4, 128 * t : 128 * t + 128] = out[4 * t : 4 * t + 4]

    psi_r, psi_i = psi_ref[0], psi_ref[1]

    def phases(x):
        return a_ref[pl.ds(x, 1), :], a_ref[pl.ds(128 + x, 1), :]

    def spread(n, carry):
        for pair in range(4):
            real, imag = [], []
            for k in range(2):
                a_r, a_i = phases(8 * n + 2 * pair + k)
                real.append(a_r * psi_r - a_i * psi_i)
                imag.append(a_r * psi_i + a_i * psi_r)
            rows = pl.ds(pl.multiple_of(64 * n + 16 * pair, 16), 16)
            p_ref[0, rows, :STICKS], p_ref[1, rows, :STICKS] = split(jnp.concatenate(real, axis=0))
            p_ref[0, rows, STICKS:], p_ref[1, rows, STICKS:] = split(jnp.concatenate(imag, axis=0))
        return carry

    lax.fori_loop(0, 14, spread, 0)

    u = dot3((p_ref[0], p_ref[1]), (t_ref[0], t_ref[1]), NT)
    v = v_ref[...].reshape(896, 128)
    for part in range(2):
        cols = slice(128 * part, 128 * part + 128)
        w_ref[0, :, cols], w_ref[1, :, cols] = split(u[:, cols] * v)

    def back_rows(n, carry):
        rows = pl.ds(pl.multiple_of(448 * n, 448), 448)
        c_ref[rows, :] = dot3((w_ref[0, rows, :], w_ref[1, rows, :]), (t_ref[0], t_ref[1]))
        return carry

    lax.fori_loop(0, 2, back_rows, 0)

    def collect(n, carry):
        w_r, w_i = carry
        for k in range(8):
            x = 8 * n + k
            a_r, a_i = phases(x)
            rows = pl.ds(pl.multiple_of(8 * x, 8), 8)
            c_r, c_i = c_ref[rows, :STICKS], c_ref[rows, STICKS:]
            w_r = w_r + (a_r * c_r + a_i * c_i)
            w_i = w_i + (a_r * c_i - a_i * c_r)
        return w_r, w_i

    zero = jnp.zeros((8, STICKS), f32)
    sums = lax.fori_loop(0, 14, collect, (zero, zero))

    outs = []
    for q in range(4):
        half = sums[q // 2][4 * (q % 2) : 4 * (q % 2) + 4]
        outs.append(jnp.concatenate([half[:, 128 * t : 128 * t + 128] for t in range(4)], axis=0))
    for p in range(4):
        out = outs[0] if p == 0 else pltpu.roll(outs[0], (-32 * p) % 128, 1)
        for q in range(1, 4):
            moved = outs[q] if p == q else pltpu.roll(outs[q], (32 * (q - p)) % 128, 1)
            out = jnp.where(group == q, moved, out)
        send_d[4 * p : 4 * p + 4] = out.reshape(4, 4, 128)
    each(lambda d: to_d(pencil_peer(d), pencil).start())
    recv_d[pencil] = send_d[slot_of(pencil)]

    def gram_rows(values, first):
        other = turned(values)

        def one(n, carry):
            for k in range(4):
                i = 4 * n + k
                member = bands_ref[i]
                for part, factor in enumerate((values, other)):
                    products = member * factor
                    folded = (products[:8] + products[8:16]) + (products[16:24] + products[24:])
                    rows = pl.ds(pl.multiple_of(128 * part + 8 * i, 8), 8)
                    sums_ref[rows, :] = folded[:, :128] + folded[:, 128:]
            return carry

        lax.fori_loop(0, 4, one, 0)
        rows_ref[first : first + 32, :] = jnp.sum(sums_ref[...].reshape(32, 8, 128), axis=1)

    def hand_on_p(d):
        to_p(chip_peer(d), chip_peer(d)).wait_recv()
        hand_p(chip_peer(d)).start()

    chips(hand_on_p)
    chips(lambda d: hand_p(lax.rem(sibling + 2 * d, BANDS)).wait_recv(), 0)
    gram_rows(own, 32)

    each(lambda d: to_d(pencil_peer(d), pencil_peer(d)).wait_recv())
    arrived = recv_d[...].reshape(64, 128)
    back = jnp.concatenate([arrived, arrived], axis=0).T
    low_half = lax.broadcasted_iota(jnp.int32, (OWN, 128), 1) < 64
    lined = jnp.concatenate(
        [jnp.where(low_half, back[64 * h : 64 * h + 32], back[64 * h + 32 : 64 * h + 64]) for h in range(2)], axis=1
    )
    own_h = kinetic * own + dot3(split(lined), (forward_ref[0], forward_ref[1]))
    bands_h_ref[band] = own_h
    for d in NEAR[::-1]:
        to_h(chip_peer(d), band).start()
    hand_h(band).start()

    gram_rows(own_h, 0)
    send_g[...] = dot_exact(jnp.ones((8, 128), f32), rows_ref[...], NT)[:1]
    each(lambda d: to_g(pencil_peer(d), pencil).start())
    recv_g[pencil] = send_g[...]
    each(lambda d: to_g(pencil_peer(d), pencil_peer(d)).wait_recv())
    row_ref[...] = jnp.sum(recv_g[...], axis=0) / float(STICKS * GRID)
    each(lambda d: to_r(band_peer(d), band).start())
    recv_r[band] = row_ref[...]
    for d in NEAR:
        to_h(chip_peer(d), chip_peer(d)).wait_recv()
        hand_h(chip_peer(d)).start()

    x_r, x_i = ritz_ref[0], ritz_ref[1]
    xt = jnp.concatenate([x_r.T, x_i.T], axis=1)
    conj = jnp.concatenate(
        [jnp.concatenate([x_r, -x_i], axis=1), jnp.concatenate([x_i, x_r], axis=1)], axis=0
    )
    each(lambda d: to_r(band_peer(d), band_peer(d)).wait_recv())
    grams = recv_r[...].reshape(BANDS, 128)
    lane = lax.broadcasted_iota(jnp.int32, (BANDS, 128), 1)
    swapped = jnp.where(lax.rem(lane, 32) < 16, -pltpu.roll(grams, 112, 1), pltpu.roll(grams, 16, 1))
    half = dot_exact(xt, jnp.concatenate([grams, swapped], axis=0))
    energy = dot_exact(half[:, :32], conj)
    metric = dot_exact(half[:, 32:64], conj)
    row16 = lax.broadcasted_iota(jnp.int32, (BANDS, 16), 0)
    diagonal = row16 == lax.broadcasted_iota(jnp.int32, (BANDS, 16), 1)
    ratio = jnp.where(diagonal, energy[:, :16] / metric[:, :16], 0.0)
    value_j = jnp.sum(ratio, axis=1, keepdims=True)
    value_i = jnp.sum(ratio, axis=0, keepdims=True)
    values_ref[...] = value_i
    spacing = value_j - value_i
    factor = spacing / jnp.maximum(spacing * spacing, (0.25 / BANDS) ** 2)
    residual_r = jnp.where(diagonal, 1.0, 0.0) - metric[:, :16]
    residual_i = -metric[:, 16:]
    update_r = jnp.where(diagonal, 0.5 * residual_r, (energy[:, :16] + value_j * residual_r) * factor)
    update_i = jnp.where(diagonal, 0.5 * residual_i, (energy[:, 16:] + value_j * residual_i) * factor)
    chosen = row16 == band
    u_r = jnp.sum(jnp.where(chosen, update_r + jnp.where(diagonal, 1.0, 0.0), 0.0), axis=0, keepdims=True)
    u_i = jnp.sum(jnp.where(chosen, update_i, 0.0), axis=0, keepdims=True)
    new_r = jnp.sum(x_r * u_r - x_i * u_i, axis=1, keepdims=True)
    new_i = jnp.sum(x_r * u_i + x_i * u_r, axis=1, keepdims=True)

    scale_ref[0] = jnp.broadcast_to(new_r, (BANDS, 256))
    scale_ref[1] = jnp.broadcast_to(new_i, (BANDS, 256))

    def add(sums, i, members):
        member = members[i]
        return sums[0] + scale_ref[0, pl.ds(i, 1), :] * member, sums[1] + scale_ref[1, pl.ds(i, 1), :] * member

    def rotated(sums):
        return narrow(sums[0] - turned(sums[1]))[:, : 2 * GRID]

    empty = (jnp.zeros((OWN, 256), f32),) * 2
    sums = empty
    for i in range(BANDS):
        sums = add(sums, i, bands_ref)
    refined_ref[0] = rotated(sums)
    sums = empty
    for d in range(8):
        sums = add(sums, chip_peer(d), bands_h_ref)
    for d in (0,) + NEAR:
        i = lax.rem(sibling + 2 * d, BANDS)
        hand_h(i).wait_recv()
        sums = add(sums, i, bands_h_ref)
    refined_h_ref[0] = rotated(sums)

    def finish(d):
        to_b(pencil_peer(d), pencil).wait_send()
        to_d(pencil_peer(d), pencil).wait_send()
        to_g(pencil_peer(d), pencil).wait_send()
        to_r(band_peer(d), band).wait_send()

    each(finish)
    chips(lambda d: to_p(chip_peer(d), band).wait_send())
    chips(lambda d: to_h(chip_peer(d), band).wait_send())
    chips(lambda d: hand_p(chip_peer(d)).wait_send(), 0)
    chips(lambda d: hand_h(chip_peer(d)).wait_send(), 0)


def emit(*refs):
    for k in range(3):
        refs[3 + k][...] = refs[k][...]


def shards(coeffs, columns, potential, ritz_vectors):
    inverse, forward = z_tables()
    vmem = pl.BlockSpec(memory_space=pltpu.VMEM)
    outs = (
        jax.ShapeDtypeStruct((1, OWN, 2 * GRID), f32),
        jax.ShapeDtypeStruct((1, OWN, 2 * GRID), f32),
        jax.ShapeDtypeStruct((1, BANDS), f32),
    )
    results = pl.pallas_call(
        kernel,
        out_shape=tuple(pltpu.VMEM(o.shape, f32) for o in outs),
        in_specs=[pl.BlockSpec(memory_space=pltpu.HBM)] * 7,
        out_specs=(vmem,) * 3,
        scratch_shapes=[
            pltpu.VMEM((1, OWN, 2 * GRID), f32),
            pltpu.VMEM((1, STICKS), jnp.int32),
            pltpu.VMEM((PLANES, GRID * GRID), f32),
            pltpu.VMEM((2, BANDS, BANDS), f32),
            pltpu.VMEM((2, 256, 256), bf16),
            pltpu.VMEM((2, 256, 256), bf16),
            pltpu.VMEM((3, 256, 128), bf16),
            pltpu.SemaphoreType.DMA((7,)),
            pltpu.VMEM((OWN, 256), f32),
            pltpu.VMEM((128, 128), f32),
            pltpu.VMEM((2, BANDS, 256), f32),
            pltpu.VMEM((16, 4, 128), f32),
            pltpu.VMEM((16, 4, 128), f32),
            pltpu.VMEM((16, 4, 128), f32),
            pltpu.VMEM((16, 4, 128), f32),
            pltpu.VMEM((2, 8, STICKS), f32),
            pltpu.VMEM((256, STICKS), f32),
            pltpu.VMEM((2, 256, 1024), bf16),
            pltpu.VMEM((GRID, 8, 128), f32),
            pltpu.VMEM((2, 896, 1024), bf16),
            pltpu.VMEM((2, 896, 256), bf16),
            pltpu.VMEM((896, 1024), f32),
            pltpu.VMEM((BANDS, OWN, 256), f32),
            pltpu.VMEM((BANDS, OWN, 256), f32),
            pltpu.VMEM((256, 128), f32),
            pltpu.VMEM((1, 128), f32),
            pltpu.VMEM((16, 1, 128), f32),
            pltpu.VMEM((1, 128), f32),
            pltpu.VMEM((16, 1, 128), f32),
        ]
        + [pltpu.SemaphoreType.DMA((16,))] * 14,
        compiler_params=pltpu.CompilerParams(
            collective_id=0, has_side_effects=True, vmem_limit_bytes=62 * 2**20
        ),
    )(
        coeffs,
        columns.reshape(1, STICKS),
        potential,
        ritz_vectors,
        jnp.asarray(inverse),
        jnp.asarray(forward),
        jnp.asarray(wave_table()),
    )
    anywhere = pl.BlockSpec(memory_space=pl.ANY)
    refined, refined_h, values = pl.pallas_call(
        emit,
        out_shape=outs,
        in_specs=[vmem] * 3,
        out_specs=(vmem,) * 3,
        compiler_params=pltpu.CompilerParams(vmem_limit_bytes=2**20),
    )(*results)
    return refined, refined_h, values.reshape(BANDS)


def solution(mesh):
    return jax.shard_map(
        shards,
        mesh=mesh,
        in_specs=(P("band", "pencil", None), P(), P("pencil", None), P()),
        out_specs=(P("band", "pencil", None), P("band", "pencil", None), P()),
        check_vma=False,
    )
```

```python
import functools

import jax
import jax.numpy as jnp
import ml_dtypes
import numpy as np
from jax import lax
from jax.experimental import pallas as pl
from jax.experimental.pallas import tpu as pltpu
from jax.sharding import PartitionSpec as P

GRID = 112
BANDS = 16
PENCILS = 16
PLANES = 7
STICKS = 512
OWN = 32
RADIUS = 28
NEAR = (1, 7, 2, 6, 3, 5, 4)


def hops(step, size):
    return min(step, size - step)


PENCIL_STEPS = sorted(
    [(dx, dy) for dx in range(4) for dy in range(4) if dx or dy], key=lambda d: -hops(d[0], 4) - hops(d[1], 4)
)
BAND_STEPS = sorted([(dz, other) for dz in range(8) for other in range(2) if dz or other], key=lambda d: -hops(d[0], 8))

f32 = jnp.float32
bf16 = jnp.bfloat16
MESH = pl.DeviceIdType.MESH
NN = (((1,), (0,)), ((), ()))
NT = (((1,), (1,)), ((), ()))


def parts_of(table, count):
    parts = []
    for _ in range(count):
        part = table.astype(ml_dtypes.bfloat16)
        parts.append(part)
        table = table - part.astype(np.float64)
    return np.stack(parts)


def wave_table():
    index = np.arange(GRID)
    angle = 2.0 * np.pi * (np.outer(index, index) % GRID) / GRID
    table = np.zeros((256, 128))
    table[:GRID, :GRID] = np.cos(angle)
    table[128 : 128 + GRID, :GRID] = np.sin(angle)
    return parts_of(table, 3)


def z_tables():
    table = np.zeros((4, PENCILS, 4, 256))
    k = np.arange(GRID)
    for p in range(PENCILS):
        for r in range(4):
            for q in range(4):
                z = 4 * (q % 2) + r
                if z >= PLANES:
                    continue
                angle = 2.0 * np.pi * ((k * (PLANES * p + z)) % GRID) / GRID
                cosine, sine = np.cos(angle), np.sin(angle)
                real = q // 2 == 0
                table[q, p, r, :GRID] = cosine if real else sine
                table[q, p, r, 128 : 128 + GRID] = -sine if real else cosine
    table = table.reshape(256, 256)
    return parts_of(table, 2), parts_of(table / float(GRID) ** 3, 2)


def split(x):
    high = x.astype(bf16)
    return high, (x - high.astype(f32)).astype(bf16)


def dot(a, b, dims=NN):
    return lax.dot_general(a, b, dims, preferred_element_type=f32)


def dot3(a, b, dims=NN):
    return dot(a[0], b[0], dims) + dot(a[0], b[1], dims) + dot(a[1], b[0], dims)


def dot_exact(a, b, dims=NN):
    return lax.dot_general(a, b, dims, precision=lax.Precision.HIGHEST, preferred_element_type=f32)


def slot_of(p):
    return lax.rem(p, 4) * 4 + lax.div(p, 4)


def frequency(index):
    return jnp.where(index < GRID // 2, index, index - GRID).astype(f32)


def wide(x):
    lane = lax.broadcasted_iota(jnp.int32, x.shape, 1)
    moved = pltpu.roll(x, 16, 1)
    return jnp.where(lane < GRID, x, jnp.where(lane < 128, 0.0, moved))


def narrow(x):
    lane = lax.broadcasted_iota(jnp.int32, x.shape, 1)
    moved = pltpu.roll(x, 240, 1)
    return jnp.where(lane < GRID, x, moved)


def turned(x):
    return jnp.concatenate([x[:, 128:], -x[:, :128]], axis=1)


def kernel(
    coeffs_hbm, columns_hbm, potential_hbm, ritz_hbm, inverse_hbm, forward_hbm, wave_hbm,
    refined_ref, refined_h_ref, values_ref,
    coeffs_ref, columns_ref, potential_ref, ritz_ref, inverse_ref, forward_ref, wave_ref, sem_in,
    pad_ref, rows_ref, scale_ref, send_b, recv_b, send_d, recv_d, psi_ref, a_ref, t_ref, v_ref, p_ref, w_ref, c_ref,
    bands_ref, bands_h_ref, sums_ref, send_g, recv_g, row_ref, recv_r,
    sem_sb, sem_rb, sem_sd, sem_rd, sem_sp, sem_fp, sem_rp, sem_sh, sem_fh, sem_rh, sem_sg, sem_rg, sem_sr, sem_rr,
):
    pencil = lax.axis_index("pencil")
    band = lax.axis_index("band")

    x_own, y_own = lax.div(pencil, 4), lax.rem(pencil, 4)

    def pencil_peer(d):
        dx, dy = PENCIL_STEPS[d - 1]
        return 4 * lax.rem(x_own + dx, 4) + lax.rem(y_own + dy, 4)

    def band_peer(d):
        dz, other = BAND_STEPS[d - 1]
        core = lax.rem(band, 2)
        return lax.rem(2 * (lax.div(band, 2) + dz), BANDS) + (1 - core if other else core)

    def each(body):
        for d in range(1, 16):
            body(d)

    def to_b(p, mine):
        return pltpu.make_async_remote_copy(
            send_b.at[p], recv_b.at[slot_of(mine)], sem_sb.at[p], sem_rb.at[mine],
            device_id=(p, band), device_id_type=MESH,
        )

    def to_d(p, mine):
        return pltpu.make_async_remote_copy(
            send_d.at[slot_of(p)], recv_d.at[mine], sem_sd.at[p], sem_rd.at[mine],
            device_id=(p, band), device_id_type=MESH,
        )

    def to_g(p, mine):
        return pltpu.make_async_remote_copy(
            send_g, recv_g.at[mine], sem_sg.at[p], sem_rg.at[mine], device_id=(p, band), device_id_type=MESH
        )

    sibling = band + 1 - 2 * lax.rem(band, 2)

    def chip_peer(d):
        return lax.rem(band + 2 * d, BANDS)

    def to_p(b, mine):
        return pltpu.make_async_remote_copy(
            bands_ref.at[mine], bands_ref.at[mine], sem_sp.at[b], sem_rp.at[mine],
            device_id=(pencil, b), device_id_type=MESH,
        )

    def hand_p(q):
        return pltpu.make_async_remote_copy(
            bands_ref.at[q], bands_ref.at[q], sem_fp.at[q], sem_rp.at[q],
            device_id=(pencil, sibling), device_id_type=MESH,
        )

    def to_h(b, mine):
        return pltpu.make_async_remote_copy(
            bands_h_ref.at[mine], bands_h_ref.at[mine], sem_sh.at[b], sem_rh.at[mine],
            device_id=(pencil, b), device_id_type=MESH,
        )

    def hand_h(q):
        return pltpu.make_async_remote_copy(
            bands_h_ref.at[q], bands_h_ref.at[q], sem_fh.at[q], sem_rh.at[q],
            device_id=(pencil, sibling), device_id_type=MESH,
        )

    def chips(body, first=1):
        def step(d, carry):
            body(d)
            return carry

        lax.fori_loop(first, 8, step, 0)

    def to_r(b, mine):
        return pltpu.make_async_remote_copy(
            row_ref, recv_r.at[mine], sem_sr.at[b], sem_rr.at[mine], device_id=(pencil, b), device_id_type=MESH
        )

    sources = (coeffs_hbm, inverse_hbm, columns_hbm, wave_hbm, potential_hbm, forward_hbm, ritz_hbm)
    targets = (coeffs_ref, inverse_ref, columns_ref, wave_ref, potential_ref, forward_ref, ritz_ref)
    loads = [pltpu.make_async_copy(a, b, sem_in.at[k]) for k, (a, b) in enumerate(zip(sources, targets))]
    barrier = pltpu.get_barrier_semaphore()
    for load in loads[:2]:
        load.start()

    def greet(d):
        pl.semaphore_signal(barrier, inc=1, device_id=(pencil_peer(d), band), device_id_type=MESH)
        pl.semaphore_signal(barrier, inc=1, device_id=(pencil, band_peer(d)), device_id_type=MESH)

    each(greet)
    for load in loads[2:]:
        load.start()
    pad_ref[...] = jnp.zeros_like(pad_ref)
    rows_ref[...] = jnp.zeros_like(rows_ref)
    for load in loads[:2]:
        load.wait()

    pad_ref[:, : 2 * GRID] = coeffs_ref[0]
    own = wide(pad_ref[...])
    bands_ref[band] = own
    group = lax.div(lax.broadcasted_iota(jnp.int32, (64, 128), 1), 32)
    copies = jnp.concatenate([own] * 4, axis=0)
    planes = dot3((inverse_ref[0], inverse_ref[1]), split(copies), NT)
    packed = planes[:64]
    for q in range(1, 4):
        packed = jnp.where(group == q, planes[64 * q : 64 * q + 64], packed)
    send_b[...] = packed.reshape(PENCILS, 4, 128)

    pl.semaphore_wait(barrier, 30)
    each(lambda d: to_b(pencil_peer(d), pencil).start())
    chips(lambda d: to_p(chip_peer(d), band).start())
    hand_p(band).start()
    recv_b[slot_of(pencil)] = send_b[pencil]
    for load in loads[2:]:
        load.wait()

    columns = columns_ref[...]
    index_x = lax.div(columns, GRID)
    index_y = lax.rem(columns, GRID)
    row = lax.broadcasted_iota(jnp.int32, (128, STICKS), 0)
    hot_x = jnp.where(row == index_x, 1.0, 0.0).astype(bf16)
    hot_y = jnp.where(row == index_y, 1.0, 0.0).astype(bf16)
    a_ref[...] = dot(wave_ref[0], hot_x) + dot(wave_ref[1], hot_x) + dot(wave_ref[2], hot_x)
    for part in range(2):
        table = dot(wave_ref[part], hot_y).astype(bf16)
        t_ref[part, :, :STICKS] = table
        t_ref[part, :128, STICKS:] = -table[128:]
        t_ref[part, 128:, STICKS:] = table[:128]
    v_ref[...] = jnp.zeros_like(v_ref)

    def lay_out(g, carry):
        block = potential_ref[:, pl.ds(pl.multiple_of(896 * g, 128), 896)]
        for k in range(8):
            v_ref[8 * g + k, :PLANES, :GRID] = block[:, GRID * k : GRID * k + GRID]
        return carry

    lax.fori_loop(0, 14, lay_out, 0)

    freq_x, freq_y = frequency(index_x), frequency(index_y)
    lateral = freq_x * freq_x + freq_y * freq_y
    stick = lax.broadcasted_iota(jnp.int32, (OWN, STICKS), 1)
    mine = stick == lax.broadcasted_iota(jnp.int32, (OWN, STICKS), 0) + OWN * pencil
    own_lateral = jnp.sum(jnp.where(mine, lateral, 0.0), axis=1, keepdims=True)
    lane = lax.broadcasted_iota(jnp.int32, (OWN, 256), 1)
    freq_z = frequency(jnp.where(lane < 128, lane, lane - 128))
    kinetic = 0.5 * (own_lateral + freq_z * freq_z) / float(RADIUS * RADIUS)

    each(lambda d: to_b(pencil_peer(d), pencil_peer(d)).wait_recv())
    got = recv_b[...].reshape(4, 16, 128)
    group = group[:16]
    for q in range(4):
        out = got[0] if q == 0 else pltpu.roll(got[0], (-32 * q) % 128, 1)
        for p in range(1, 4):
            moved = got[p] if p == q else pltpu.roll(got[p], (32 * (p - q)) % 128, 1)
            out = jnp.where(group == p, moved, out)
        for t in range(4):
            psi_ref[q // 2, 4 * (q % 2) : 4 * (q % 2) + 4, 128 * t : 128 * t + 128] = out[4 * t : 4 * t + 4]

    psi_r, psi_i = psi_ref[0], psi_ref[1]

    def phases(x):
        return a_ref[pl.ds(x, 1), :], a_ref[pl.ds(128 + x, 1), :]

    def spread(n, carry):
        for pair in range(4):
            real, imag = [], []
            for k in range(2):
                a_r, a_i = phases(8 * n + 2 * pair + k)
                real.append(a_r * psi_r - a_i * psi_i)
                imag.append(a_r * psi_i + a_i * psi_r)
            rows = pl.ds(pl.multiple_of(64 * n + 16 * pair, 16), 16)
            p_ref[0, rows, :STICKS], p_ref[1, rows, :STICKS] = split(jnp.concatenate(real, axis=0))
            p_ref[0, rows, STICKS:], p_ref[1, rows, STICKS:] = split(jnp.concatenate(imag, axis=0))
        return carry

    lax.fori_loop(0, 14, spread, 0)

    u = dot3((p_ref[0], p_ref[1]), (t_ref[0], t_ref[1]), NT)
    v = v_ref[...].reshape(896, 128)
    for part in range(2):
        cols = slice(128 * part, 128 * part + 128)
        w_ref[0, :, cols], w_ref[1, :, cols] = split(u[:, cols] * v)

    def back_rows(n, carry):
        rows = pl.ds(pl.multiple_of(448 * n, 448), 448)
        c_ref[rows, :] = dot3((w_ref[0, rows, :], w_ref[1, rows, :]), (t_ref[0], t_ref[1]))
        return carry

    lax.fori_loop(0, 2, back_rows, 0)

    def collect(n, carry):
        w_r, w_i = carry
        for k in range(8):
            x = 8 * n + k
            a_r, a_i = phases(x)
            rows = pl.ds(pl.multiple_of(8 * x, 8), 8)
            c_r, c_i = c_ref[rows, :STICKS], c_ref[rows, STICKS:]
            w_r = w_r + (a_r * c_r + a_i * c_i)
            w_i = w_i + (a_r * c_i - a_i * c_r)
        return w_r, w_i

    zero = jnp.zeros((8, STICKS), f32)
    sums = lax.fori_loop(0, 14, collect, (zero, zero))

    outs = []
    for q in range(4):
        half = sums[q // 2][4 * (q % 2) : 4 * (q % 2) + 4]
        outs.append(jnp.concatenate([half[:, 128 * t : 128 * t + 128] for t in range(4)], axis=0))
    for p in range(4):
        out = outs[0] if p == 0 else pltpu.roll(outs[0], (-32 * p) % 128, 1)
        for q in range(1, 4):
            moved = outs[q] if p == q else pltpu.roll(outs[q], (32 * (q - p)) % 128, 1)
            out = jnp.where(group == q, moved, out)
        send_d[4 * p : 4 * p + 4] = out.reshape(4, 4, 128)
    each(lambda d: to_d(pencil_peer(d), pencil).start())
    recv_d[pencil] = send_d[slot_of(pencil)]

    def gram_rows(values, first):
        other = turned(values)

        def one(n, carry):
            for k in range(4):
                i = 4 * n + k
                member = bands_ref[i]
                for part, factor in enumerate((values, other)):
                    products = member * factor
                    folded = (products[:8] + products[8:16]) + (products[16:24] + products[24:])
                    rows = pl.ds(pl.multiple_of(128 * part + 8 * i, 8), 8)
                    sums_ref[rows, :] = folded[:, :128] + folded[:, 128:]
            return carry

        lax.fori_loop(0, 4, one, 0)
        rows_ref[first : first + 32, :] = jnp.sum(sums_ref[...].reshape(32, 8, 128), axis=1)

    def hand_on_p(d):
        to_p(chip_peer(d), chip_peer(d)).wait_recv()
        hand_p(chip_peer(d)).start()

    chips(hand_on_p)
    chips(lambda d: hand_p(lax.rem(sibling + 2 * d, BANDS)).wait_recv(), 0)
    gram_rows(own, 32)

    each(lambda d: to_b(pencil_peer(d), pencil).wait_send())
    chips(lambda d: to_p(chip_peer(d), band).wait_send())
    chips(lambda d: hand_p(chip_peer(d)).wait_send(), 0)
    each(lambda d: to_d(pencil_peer(d), pencil_peer(d)).wait_recv())
    arrived = recv_d[...].reshape(64, 128)
    back = jnp.concatenate([arrived, arrived], axis=0).T
    low_half = lax.broadcasted_iota(jnp.int32, (OWN, 128), 1) < 64
    lined = jnp.concatenate(
        [jnp.where(low_half, back[64 * h : 64 * h + 32], back[64 * h + 32 : 64 * h + 64]) for h in range(2)], axis=1
    )
    own_h = kinetic * own + dot3(split(lined), (forward_ref[0], forward_ref[1]))
    bands_h_ref[band] = own_h
    for d in NEAR[::-1]:
        to_h(chip_peer(d), band).start()
    hand_h(band).start()

    gram_rows(own_h, 0)
    send_g[...] = dot_exact(jnp.ones((8, 128), f32), rows_ref[...], NT)[:1]
    each(lambda d: to_g(pencil_peer(d), pencil).start())
    recv_g[pencil] = send_g[...]
    each(lambda d: to_d(pencil_peer(d), pencil).wait_send())
    each(lambda d: to_g(pencil_peer(d), pencil_peer(d)).wait_recv())
    row_ref[...] = jnp.sum(recv_g[...], axis=0) / float(STICKS * GRID)
    each(lambda d: to_r(band_peer(d), band).start())
    recv_r[band] = row_ref[...]
    for d in NEAR:
        to_h(chip_peer(d), chip_peer(d)).wait_recv()
        hand_h(chip_peer(d)).start()

    x_r, x_i = ritz_ref[0], ritz_ref[1]
    xt = jnp.concatenate([x_r.T, x_i.T], axis=1)
    conj = jnp.concatenate(
        [jnp.concatenate([x_r, -x_i], axis=1), jnp.concatenate([x_i, x_r], axis=1)], axis=0
    )
    each(lambda d: to_g(pencil_peer(d), pencil).wait_send())
    chips(lambda d: to_h(chip_peer(d), band).wait_send())
    each(lambda d: to_r(band_peer(d), band).wait_send())
    each(lambda d: to_r(band_peer(d), band_peer(d)).wait_recv())
    grams = recv_r[...].reshape(BANDS, 128)
    lane = lax.broadcasted_iota(jnp.int32, (BANDS, 128), 1)
    swapped = jnp.where(lax.rem(lane, 32) < 16, -pltpu.roll(grams, 112, 1), pltpu.roll(grams, 16, 1))
    half = dot_exact(xt, jnp.concatenate([grams, swapped], axis=0))
    pair = dot_exact(jnp.concatenate([half[:, :32], half[:, 32:64]], axis=0), conj)
    energy, metric = pair[:BANDS], pair[BANDS:]
    row16 = lax.broadcasted_iota(jnp.int32, (BANDS, 16), 0)
    diagonal = row16 == lax.broadcasted_iota(jnp.int32, (BANDS, 16), 1)
    ratio = jnp.where(diagonal, energy[:, :16] / metric[:, :16], 0.0)
    value_j = jnp.sum(ratio, axis=1, keepdims=True)
    value_i = jnp.sum(ratio, axis=0, keepdims=True)
    values_ref[...] = value_i
    spacing = value_j - value_i
    factor = spacing / jnp.maximum(spacing * spacing, (0.25 / BANDS) ** 2)
    residual_r = jnp.where(diagonal, 1.0, 0.0) - metric[:, :16]
    residual_i = -metric[:, 16:]
    update_r = jnp.where(diagonal, 0.5 * residual_r, (energy[:, :16] + value_j * residual_r) * factor)
    update_i = jnp.where(diagonal, 0.5 * residual_i, (energy[:, 16:] + value_j * residual_i) * factor)
    chosen = row16 == band
    u_r = jnp.sum(jnp.where(chosen, update_r + jnp.where(diagonal, 1.0, 0.0), 0.0), axis=0, keepdims=True)
    u_i = jnp.sum(jnp.where(chosen, update_i, 0.0), axis=0, keepdims=True)
    new_r = jnp.sum(x_r * u_r - x_i * u_i, axis=1, keepdims=True)
    new_i = jnp.sum(x_r * u_i + x_i * u_r, axis=1, keepdims=True)

    scale_ref[0] = jnp.broadcast_to(new_r, (BANDS, 256))
    scale_ref[1] = jnp.broadcast_to(new_i, (BANDS, 256))

    def add(sums, i, members):
        member = members[i]
        return sums[0] + scale_ref[0, pl.ds(i, 1), :] * member, sums[1] + scale_ref[1, pl.ds(i, 1), :] * member

    def rotated(sums):
        return narrow(sums[0] - turned(sums[1]))[:, : 2 * GRID]

    empty = (jnp.zeros((OWN, 256), f32),) * 2
    sums = empty
    for i in range(BANDS):
        sums = add(sums, i, bands_ref)
    refined_ref[0] = rotated(sums)
    sums = empty
    for d in range(8):
        sums = add(sums, chip_peer(d), bands_h_ref)
    for d in (0,) + NEAR:
        i = lax.rem(sibling + 2 * d, BANDS)
        hand_h(i).wait_recv()
        sums = add(sums, i, bands_h_ref)
    refined_h_ref[0] = rotated(sums)

    chips(lambda d: hand_h(chip_peer(d)).wait_send(), 0)


def emit(*refs):
    for k in range(3):
        refs[3 + k][...] = refs[k][...]


def shards(coeffs, columns, potential, ritz_vectors):
    inverse, forward = z_tables()
    vmem = pl.BlockSpec(memory_space=pltpu.VMEM)
    outs = (
        jax.ShapeDtypeStruct((1, OWN, 2 * GRID), f32),
        jax.ShapeDtypeStruct((1, OWN, 2 * GRID), f32),
        jax.ShapeDtypeStruct((1, BANDS), f32),
    )
    results = pl.pallas_call(
        kernel,
        out_shape=tuple(pltpu.VMEM(o.shape, f32) for o in outs),
        in_specs=[pl.BlockSpec(memory_space=pltpu.HBM)] * 7,
        out_specs=(vmem,) * 3,
        scratch_shapes=[
            pltpu.VMEM((1, OWN, 2 * GRID), f32),
            pltpu.VMEM((1, STICKS), jnp.int32),
            pltpu.VMEM((PLANES, GRID * GRID), f32),
            pltpu.VMEM((2, BANDS, BANDS), f32),
            pltpu.VMEM((2, 256, 256), bf16),
            pltpu.VMEM((2, 256, 256), bf16),
            pltpu.VMEM((3, 256, 128), bf16),
            pltpu.SemaphoreType.DMA((7,)),
            pltpu.VMEM((OWN, 256), f32),
            pltpu.VMEM((128, 128), f32),
            pltpu.VMEM((2, BANDS, 256), f32),
            pltpu.VMEM((16, 4, 128), f32),
            pltpu.VMEM((16, 4, 128), f32),
            pltpu.VMEM((16, 4, 128), f32),
            pltpu.VMEM((16, 4, 128), f32),
            pltpu.VMEM((2, 8, STICKS), f32),
            pltpu.VMEM((256, STICKS), f32),
            pltpu.VMEM((2, 256, 1024), bf16),
            pltpu.VMEM((GRID, 8, 128), f32),
            pltpu.VMEM((2, 896, 1024), bf16),
            pltpu.VMEM((2, 896, 256), bf16),
            pltpu.VMEM((896, 1024), f32),
            pltpu.VMEM((BANDS, OWN, 256), f32),
            pltpu.VMEM((BANDS, OWN, 256), f32),
            pltpu.VMEM((256, 128), f32),
            pltpu.VMEM((1, 128), f32),
            pltpu.VMEM((16, 1, 128), f32),
            pltpu.VMEM((1, 128), f32),
            pltpu.VMEM((16, 1, 128), f32),
        ]
        + [pltpu.SemaphoreType.DMA((16,))] * 14,
        compiler_params=pltpu.CompilerParams(
            collective_id=0, has_side_effects=True, vmem_limit_bytes=62 * 2**20
        ),
    )(
        coeffs,
        columns.reshape(1, STICKS),
        potential,
        ritz_vectors,
        jnp.asarray(inverse),
        jnp.asarray(forward),
        jnp.asarray(wave_table()),
    )
    anywhere = pl.BlockSpec(memory_space=pl.ANY)
    refined, refined_h, values = pl.pallas_call(
        emit,
        out_shape=outs,
        in_specs=[vmem] * 3,
        out_specs=(vmem,) * 3,
        compiler_params=pltpu.CompilerParams(vmem_limit_bytes=2**20),
    )(*results)
    return refined, refined_h, values.reshape(BANDS)


def solution(mesh):
    return jax.shard_map(
        shards,
        mesh=mesh,
        in_specs=(P("band", "pencil", None), P(), P("pencil", None), P()),
        out_specs=(P("band", "pencil", None), P("band", "pencil", None), P()),
        check_vma=False,
    )
```

```python
import functools

import jax
import jax.numpy as jnp
import ml_dtypes
import numpy as np
from jax import lax
from jax.experimental import pallas as pl
from jax.experimental.pallas import tpu as pltpu
from jax.sharding import PartitionSpec as P

GRID = 112
BANDS = 16
PENCILS = 16
PLANES = 7
STICKS = 512
OWN = 32
RADIUS = 28
NEAR = (1, 7, 2, 6, 3, 5, 4)


def hops(step, size):
    return min(step, size - step)


PENCIL_STEPS = sorted(
    [(dx, dy) for dx in range(4) for dy in range(4) if dx or dy], key=lambda d: -hops(d[0], 4) - hops(d[1], 4)
)
BAND_STEPS = sorted([(dz, other) for dz in range(8) for other in range(2) if dz or other], key=lambda d: -hops(d[0], 8))

f32 = jnp.float32
bf16 = jnp.bfloat16
MESH = pl.DeviceIdType.MESH
NN = (((1,), (0,)), ((), ()))
NT = (((1,), (1,)), ((), ()))


def parts_of(table, count):
    parts = []
    for _ in range(count):
        part = table.astype(ml_dtypes.bfloat16)
        parts.append(part)
        table = table - part.astype(np.float64)
    return np.stack(parts)


def wave_table():
    index = np.arange(GRID)
    angle = 2.0 * np.pi * (np.outer(index, index) % GRID) / GRID
    table = np.zeros((256, 128))
    table[:GRID, :GRID] = np.cos(angle)
    table[128 : 128 + GRID, :GRID] = np.sin(angle)
    return parts_of(table, 3)


def z_tables():
    table = np.zeros((4, PENCILS, 4, 256))
    k = np.arange(GRID)
    for p in range(PENCILS):
        for r in range(4):
            for q in range(4):
                z = 4 * (q % 2) + r
                if z >= PLANES:
                    continue
                angle = 2.0 * np.pi * ((k * (PLANES * p + z)) % GRID) / GRID
                cosine, sine = np.cos(angle), np.sin(angle)
                real = q // 2 == 0
                table[q, p, r, :GRID] = cosine if real else sine
                table[q, p, r, 128 : 128 + GRID] = -sine if real else cosine
    table = table.reshape(256, 256)
    return parts_of(table, 2), parts_of(table / float(GRID) ** 3, 2)


def split(x):
    high = x.astype(bf16)
    return high, (x - high.astype(f32)).astype(bf16)


def dot(a, b, dims=NN):
    return lax.dot_general(a, b, dims, preferred_element_type=f32)


def dot3(a, b, dims=NN):
    return dot(a[0], b[0], dims) + dot(a[0], b[1], dims) + dot(a[1], b[0], dims)


def dot_exact(a, b, dims=NN):
    return lax.dot_general(a, b, dims, precision=lax.Precision.HIGHEST, preferred_element_type=f32)


def slot_of(p):
    return lax.rem(p, 4) * 4 + lax.div(p, 4)


def frequency(index):
    return jnp.where(index < GRID // 2, index, index - GRID).astype(f32)


def wide(x):
    lane = lax.broadcasted_iota(jnp.int32, x.shape, 1)
    moved = pltpu.roll(x, 16, 1)
    return jnp.where(lane < GRID, x, jnp.where(lane < 128, 0.0, moved))


def narrow(x):
    lane = lax.broadcasted_iota(jnp.int32, x.shape, 1)
    moved = pltpu.roll(x, 240, 1)
    return jnp.where(lane < GRID, x, moved)


def turned(x):
    return jnp.concatenate([x[:, 128:], -x[:, :128]], axis=1)


def kernel(
    coeffs_hbm, columns_hbm, potential_hbm, ritz_hbm, inverse_hbm, forward_hbm, wave_hbm,
    refined_ref, refined_h_ref, values_ref,
    coeffs_ref, columns_ref, potential_ref, ritz_ref, inverse_ref, forward_ref, wave_ref, sem_in,
    pad_ref, rows_ref, scale_ref, send_b, recv_b, send_d, recv_d, psi_ref, a_ref, t_ref, v_ref, p_ref, w_ref, c_ref,
    bands_ref, bands_h_ref, sums_ref, send_g, recv_g, row_ref, recv_r,
    sem_sb, sem_rb, sem_sd, sem_rd, sem_sp, sem_fp, sem_rp, sem_sh, sem_fh, sem_rh, sem_sg, sem_rg, sem_sr, sem_rr,
):
    pencil = lax.axis_index("pencil")
    band = lax.axis_index("band")

    x_own, y_own = lax.div(pencil, 4), lax.rem(pencil, 4)

    def pencil_peer(d):
        dx, dy = PENCIL_STEPS[d - 1]
        return 4 * lax.rem(x_own + dx, 4) + lax.rem(y_own + dy, 4)

    def band_peer(d):
        dz, other = BAND_STEPS[d - 1]
        core = lax.rem(band, 2)
        return lax.rem(2 * (lax.div(band, 2) + dz), BANDS) + (1 - core if other else core)

    def each(body):
        for d in range(1, 16):
            body(d)

    def to_b(p, mine):
        return pltpu.make_async_remote_copy(
            send_b.at[p], recv_b.at[slot_of(mine)], sem_sb.at[p], sem_rb.at[mine],
            device_id=(p, band), device_id_type=MESH,
        )

    def to_d(p, mine):
        return pltpu.make_async_remote_copy(
            send_d.at[slot_of(p)], recv_d.at[mine], sem_sd.at[p], sem_rd.at[mine],
            device_id=(p, band), device_id_type=MESH,
        )

    def to_g(p, mine):
        return pltpu.make_async_remote_copy(
            send_g, recv_g.at[mine], sem_sg.at[p], sem_rg.at[mine], device_id=(p, band), device_id_type=MESH
        )

    sibling = band + 1 - 2 * lax.rem(band, 2)

    def chip_peer(d):
        return lax.rem(band + 2 * d, BANDS)

    def to_p(b, mine):
        return pltpu.make_async_remote_copy(
            bands_ref.at[mine], bands_ref.at[mine], sem_sp.at[b], sem_rp.at[mine],
            device_id=(pencil, b), device_id_type=MESH,
        )

    def hand_p(q):
        return pltpu.make_async_remote_copy(
            bands_ref.at[q], bands_ref.at[q], sem_fp.at[q], sem_rp.at[q],
            device_id=(pencil, sibling), device_id_type=MESH,
        )

    def to_h(b, mine):
        return pltpu.make_async_remote_copy(
            bands_h_ref.at[mine], bands_h_ref.at[mine], sem_sh.at[b], sem_rh.at[mine],
            device_id=(pencil, b), device_id_type=MESH,
        )

    def hand_h(q):
        return pltpu.make_async_remote_copy(
            bands_h_ref.at[q], bands_h_ref.at[q], sem_fh.at[q], sem_rh.at[q],
            device_id=(pencil, sibling), device_id_type=MESH,
        )

    def chips(body, first=1):
        def step(d, carry):
            body(d)
            return carry

        lax.fori_loop(first, 8, step, 0)

    def to_r(b, mine):
        return pltpu.make_async_remote_copy(
            row_ref, recv_r.at[mine], sem_sr.at[b], sem_rr.at[mine], device_id=(pencil, b), device_id_type=MESH
        )

    sources = (coeffs_hbm, inverse_hbm, columns_hbm, wave_hbm, potential_hbm, forward_hbm, ritz_hbm)
    targets = (coeffs_ref, inverse_ref, columns_ref, wave_ref, potential_ref, forward_ref, ritz_ref)
    loads = [pltpu.make_async_copy(a, b, sem_in.at[k]) for k, (a, b) in enumerate(zip(sources, targets))]
    barrier = pltpu.get_barrier_semaphore()
    for load in loads[:2]:
        load.start()

    def greet(d):
        pl.semaphore_signal(barrier, inc=1, device_id=(pencil_peer(d), band), device_id_type=MESH)
        pl.semaphore_signal(barrier, inc=1, device_id=(pencil, band_peer(d)), device_id_type=MESH)

    each(greet)
    for load in loads[2:]:
        load.start()
    pad_ref[...] = jnp.zeros_like(pad_ref)
    rows_ref[...] = jnp.zeros_like(rows_ref)
    for load in loads[:2]:
        load.wait()

    pad_ref[:, : 2 * GRID] = coeffs_ref[0]
    own = wide(pad_ref[...])
    bands_ref[band] = own
    group = lax.div(lax.broadcasted_iota(jnp.int32, (64, 128), 1), 32)
    copies = jnp.concatenate([own] * 4, axis=0)
    planes = dot3((inverse_ref[0], inverse_ref[1]), split(copies), NT)
    packed = planes[:64]
    for q in range(1, 4):
        packed = jnp.where(group == q, planes[64 * q : 64 * q + 64], packed)
    send_b[...] = packed.reshape(PENCILS, 4, 128)

    pl.semaphore_wait(barrier, 30)
    each(lambda d: to_b(pencil_peer(d), pencil).start())
    recv_b[slot_of(pencil)] = send_b[pencil]
    for load in loads[2:]:
        load.wait()

    columns = columns_ref[...]
    index_x = lax.div(columns, GRID)
    index_y = lax.rem(columns, GRID)
    row = lax.broadcasted_iota(jnp.int32, (128, STICKS), 0)
    hot_x = jnp.where(row == index_x, 1.0, 0.0).astype(bf16)
    hot_y = jnp.where(row == index_y, 1.0, 0.0).astype(bf16)
    a_ref[...] = dot(wave_ref[0], hot_x) + dot(wave_ref[1], hot_x) + dot(wave_ref[2], hot_x)
    for part in range(2):
        table = dot(wave_ref[part], hot_y).astype(bf16)
        t_ref[part, :, :STICKS] = table
        t_ref[part, :128, STICKS:] = -table[128:]
        t_ref[part, 128:, STICKS:] = table[:128]
    v_ref[...] = jnp.zeros_like(v_ref)

    def lay_out(g, carry):
        block = potential_ref[:, pl.ds(pl.multiple_of(896 * g, 128), 896)]
        for k in range(8):
            v_ref[8 * g + k, :PLANES, :GRID] = block[:, GRID * k : GRID * k + GRID]
        return carry

    lax.fori_loop(0, 14, lay_out, 0)

    chips(lambda d: to_p(chip_peer(d), band).start())
    hand_p(band).start()
    freq_x, freq_y = frequency(index_x), frequency(index_y)
    lateral = freq_x * freq_x + freq_y * freq_y
    stick = lax.broadcasted_iota(jnp.int32, (OWN, STICKS), 1)
    mine = stick == lax.broadcasted_iota(jnp.int32, (OWN, STICKS), 0) + OWN * pencil
    own_lateral = jnp.sum(jnp.where(mine, lateral, 0.0), axis=1, keepdims=True)
    lane = lax.broadcasted_iota(jnp.int32, (OWN, 256), 1)
    freq_z = frequency(jnp.where(lane < 128, lane, lane - 128))
    kinetic = 0.5 * (own_lateral + freq_z * freq_z) / float(RADIUS * RADIUS)

    each(lambda d: to_b(pencil_peer(d), pencil_peer(d)).wait_recv())
    got = recv_b[...].reshape(4, 16, 128)
    group = group[:16]
    for q in range(4):
        out = got[0] if q == 0 else pltpu.roll(got[0], (-32 * q) % 128, 1)
        for p in range(1, 4):
            moved = got[p] if p == q else pltpu.roll(got[p], (32 * (p - q)) % 128, 1)
            out = jnp.where(group == p, moved, out)
        for t in range(4):
            psi_ref[q // 2, 4 * (q % 2) : 4 * (q % 2) + 4, 128 * t : 128 * t + 128] = out[4 * t : 4 * t + 4]

    psi_r, psi_i = psi_ref[0], psi_ref[1]

    def phases(x):
        return a_ref[pl.ds(x, 1), :], a_ref[pl.ds(128 + x, 1), :]

    def spread(n, carry):
        for pair in range(4):
            real, imag = [], []
            for k in range(2):
                a_r, a_i = phases(8 * n + 2 * pair + k)
                real.append(a_r * psi_r - a_i * psi_i)
                imag.append(a_r * psi_i + a_i * psi_r)
            rows = pl.ds(pl.multiple_of(64 * n + 16 * pair, 16), 16)
            p_ref[0, rows, :STICKS], p_ref[1, rows, :STICKS] = split(jnp.concatenate(real, axis=0))
            p_ref[0, rows, STICKS:], p_ref[1, rows, STICKS:] = split(jnp.concatenate(imag, axis=0))
        return carry

    lax.fori_loop(0, 14, spread, 0)

    u = dot3((p_ref[0], p_ref[1]), (t_ref[0], t_ref[1]), NT)
    v = v_ref[...].reshape(896, 128)
    for part in range(2):
        cols = slice(128 * part, 128 * part + 128)
        w_ref[0, :, cols], w_ref[1, :, cols] = split(u[:, cols] * v)

    def back_rows(n, carry):
        rows = pl.ds(pl.multiple_of(448 * n, 448), 448)
        c_ref[rows, :] = dot3((w_ref[0, rows, :], w_ref[1, rows, :]), (t_ref[0], t_ref[1]))
        return carry

    lax.fori_loop(0, 2, back_rows, 0)

    def collect(n, carry):
        w_r, w_i = carry
        for k in range(8):
            x = 8 * n + k
            a_r, a_i = phases(x)
            rows = pl.ds(pl.multiple_of(8 * x, 8), 8)
            c_r, c_i = c_ref[rows, :STICKS], c_ref[rows, STICKS:]
            w_r = w_r + (a_r * c_r + a_i * c_i)
            w_i = w_i + (a_r * c_i - a_i * c_r)
        return w_r, w_i

    zero = jnp.zeros((8, STICKS), f32)
    sums = lax.fori_loop(0, 14, collect, (zero, zero))

    outs = []
    for q in range(4):
        half = sums[q // 2][4 * (q % 2) : 4 * (q % 2) + 4]
        outs.append(jnp.concatenate([half[:, 128 * t : 128 * t + 128] for t in range(4)], axis=0))
    for p in range(4):
        out = outs[0] if p == 0 else pltpu.roll(outs[0], (-32 * p) % 128, 1)
        for q in range(1, 4):
            moved = outs[q] if p == q else pltpu.roll(outs[q], (32 * (q - p)) % 128, 1)
            out = jnp.where(group == q, moved, out)
        send_d[4 * p : 4 * p + 4] = out.reshape(4, 4, 128)
    each(lambda d: to_d(pencil_peer(d), pencil).start())
    recv_d[pencil] = send_d[slot_of(pencil)]

    def gram_rows(values, first):
        other = turned(values)

        def one(n, carry):
            for k in range(4):
                i = 4 * n + k
                member = bands_ref[i]
                for part, factor in enumerate((values, other)):
                    products = member * factor
                    folded = (products[:8] + products[8:16]) + (products[16:24] + products[24:])
                    rows = pl.ds(pl.multiple_of(128 * part + 8 * i, 8), 8)
                    sums_ref[rows, :] = folded[:, :128] + folded[:, 128:]
            return carry

        lax.fori_loop(0, 4, one, 0)
        rows_ref[first : first + 32, :] = jnp.sum(sums_ref[...].reshape(32, 8, 128), axis=1)

    def hand_on_p(d):
        to_p(chip_peer(d), chip_peer(d)).wait_recv()
        hand_p(chip_peer(d)).start()

    chips(hand_on_p)
    chips(lambda d: hand_p(lax.rem(sibling + 2 * d, BANDS)).wait_recv(), 0)
    gram_rows(own, 32)

    each(lambda d: to_b(pencil_peer(d), pencil).wait_send())
    chips(lambda d: to_p(chip_peer(d), band).wait_send())
    chips(lambda d: hand_p(chip_peer(d)).wait_send(), 0)
    each(lambda d: to_d(pencil_peer(d), pencil_peer(d)).wait_recv())
    arrived = recv_d[...].reshape(64, 128)
    back = jnp.concatenate([arrived, arrived], axis=0).T
    low_half = lax.broadcasted_iota(jnp.int32, (OWN, 128), 1) < 64
    lined = jnp.concatenate(
        [jnp.where(low_half, back[64 * h : 64 * h + 32], back[64 * h + 32 : 64 * h + 64]) for h in range(2)], axis=1
    )
    own_h = kinetic * own + dot3(split(lined), (forward_ref[0], forward_ref[1]))
    bands_h_ref[band] = own_h
    for d in NEAR[::-1]:
        to_h(chip_peer(d), band).start()
    hand_h(band).start()

    gram_rows(own_h, 0)
    send_g[...] = dot_exact(jnp.ones((8, 128), f32), rows_ref[...], NT)[:1]
    each(lambda d: to_g(pencil_peer(d), pencil).start())
    recv_g[pencil] = send_g[...]
    each(lambda d: to_d(pencil_peer(d), pencil).wait_send())
    each(lambda d: to_g(pencil_peer(d), pencil_peer(d)).wait_recv())
    row_ref[...] = jnp.sum(recv_g[...], axis=0) / float(STICKS * GRID)
    each(lambda d: to_r(band_peer(d), band).start())
    recv_r[band] = row_ref[...]
    for d in NEAR:
        to_h(chip_peer(d), chip_peer(d)).wait_recv()
        hand_h(chip_peer(d)).start()

    x_r, x_i = ritz_ref[0], ritz_ref[1]
    xt = jnp.concatenate([x_r.T, x_i.T], axis=1)
    conj = jnp.concatenate(
        [jnp.concatenate([x_r, -x_i], axis=1), jnp.concatenate([x_i, x_r], axis=1)], axis=0
    )
    each(lambda d: to_g(pencil_peer(d), pencil).wait_send())
    chips(lambda d: to_h(chip_peer(d), band).wait_send())
    each(lambda d: to_r(band_peer(d), band).wait_send())
    each(lambda d: to_r(band_peer(d), band_peer(d)).wait_recv())
    grams = recv_r[...].reshape(BANDS, 128)
    lane = lax.broadcasted_iota(jnp.int32, (BANDS, 128), 1)
    swapped = jnp.where(lax.rem(lane, 32) < 16, -pltpu.roll(grams, 112, 1), pltpu.roll(grams, 16, 1))
    half = dot_exact(xt, jnp.concatenate([grams, swapped], axis=0))
    pair = dot_exact(jnp.concatenate([half[:, :32], half[:, 32:64]], axis=0), conj)
    energy, metric = pair[:BANDS], pair[BANDS:]
    row16 = lax.broadcasted_iota(jnp.int32, (BANDS, 16), 0)
    diagonal = row16 == lax.broadcasted_iota(jnp.int32, (BANDS, 16), 1)
    ratio = jnp.where(diagonal, energy[:, :16] / metric[:, :16], 0.0)
    value_j = jnp.sum(ratio, axis=1, keepdims=True)
    value_i = jnp.sum(ratio, axis=0, keepdims=True)
    values_ref[...] = value_i
    spacing = value_j - value_i
    factor = spacing / jnp.maximum(spacing * spacing, (0.25 / BANDS) ** 2)
    residual_r = jnp.where(diagonal, 1.0, 0.0) - metric[:, :16]
    residual_i = -metric[:, 16:]
    update_r = jnp.where(diagonal, 0.5 * residual_r, (energy[:, :16] + value_j * residual_r) * factor)
    update_i = jnp.where(diagonal, 0.5 * residual_i, (energy[:, 16:] + value_j * residual_i) * factor)
    chosen = row16 == band
    u_r = jnp.sum(jnp.where(chosen, update_r + jnp.where(diagonal, 1.0, 0.0), 0.0), axis=0, keepdims=True)
    u_i = jnp.sum(jnp.where(chosen, update_i, 0.0), axis=0, keepdims=True)
    new_r = jnp.sum(x_r * u_r - x_i * u_i, axis=1, keepdims=True)
    new_i = jnp.sum(x_r * u_i + x_i * u_r, axis=1, keepdims=True)

    scale_ref[0] = jnp.broadcast_to(new_r, (BANDS, 256))
    scale_ref[1] = jnp.broadcast_to(new_i, (BANDS, 256))

    def add(sums, i, members):
        member = members[i]
        return sums[0] + scale_ref[0, pl.ds(i, 1), :] * member, sums[1] + scale_ref[1, pl.ds(i, 1), :] * member

    def rotated(sums):
        return narrow(sums[0] - turned(sums[1]))[:, : 2 * GRID]

    empty = (jnp.zeros((OWN, 256), f32),) * 2
    sums = empty
    for i in range(BANDS):
        sums = add(sums, i, bands_ref)
    refined_ref[0] = rotated(sums)
    sums = empty
    for d in range(8):
        sums = add(sums, chip_peer(d), bands_h_ref)
    for d in (0,) + NEAR:
        i = lax.rem(sibling + 2 * d, BANDS)
        hand_h(i).wait_recv()
        sums = add(sums, i, bands_h_ref)
    refined_h_ref[0] = rotated(sums)

    chips(lambda d: hand_h(chip_peer(d)).wait_send(), 0)


def emit(*refs):
    for k in range(3):
        refs[3 + k][...] = refs[k][...]


def shards(coeffs, columns, potential, ritz_vectors):
    inverse, forward = z_tables()
    vmem = pl.BlockSpec(memory_space=pltpu.VMEM)
    outs = (
        jax.ShapeDtypeStruct((1, OWN, 2 * GRID), f32),
        jax.ShapeDtypeStruct((1, OWN, 2 * GRID), f32),
        jax.ShapeDtypeStruct((1, BANDS), f32),
    )
    results = pl.pallas_call(
        kernel,
        out_shape=tuple(pltpu.VMEM(o.shape, f32) for o in outs),
        in_specs=[pl.BlockSpec(memory_space=pltpu.HBM)] * 7,
        out_specs=(vmem,) * 3,
        scratch_shapes=[
            pltpu.VMEM((1, OWN, 2 * GRID), f32),
            pltpu.VMEM((1, STICKS), jnp.int32),
            pltpu.VMEM((PLANES, GRID * GRID), f32),
            pltpu.VMEM((2, BANDS, BANDS), f32),
            pltpu.VMEM((2, 256, 256), bf16),
            pltpu.VMEM((2, 256, 256), bf16),
            pltpu.VMEM((3, 256, 128), bf16),
            pltpu.SemaphoreType.DMA((7,)),
            pltpu.VMEM((OWN, 256), f32),
            pltpu.VMEM((128, 128), f32),
            pltpu.VMEM((2, BANDS, 256), f32),
            pltpu.VMEM((16, 4, 128), f32),
            pltpu.VMEM((16, 4, 128), f32),
            pltpu.VMEM((16, 4, 128), f32),
            pltpu.VMEM((16, 4, 128), f32),
            pltpu.VMEM((2, 8, STICKS), f32),
            pltpu.VMEM((256, STICKS), f32),
            pltpu.VMEM((2, 256, 1024), bf16),
            pltpu.VMEM((GRID, 8, 128), f32),
            pltpu.VMEM((2, 896, 1024), bf16),
            pltpu.VMEM((2, 896, 256), bf16),
            pltpu.VMEM((896, 1024), f32),
            pltpu.VMEM((BANDS, OWN, 256), f32),
            pltpu.VMEM((BANDS, OWN, 256), f32),
            pltpu.VMEM((256, 128), f32),
            pltpu.VMEM((1, 128), f32),
            pltpu.VMEM((16, 1, 128), f32),
            pltpu.VMEM((1, 128), f32),
            pltpu.VMEM((16, 1, 128), f32),
        ]
        + [pltpu.SemaphoreType.DMA((16,))] * 14,
        compiler_params=pltpu.CompilerParams(
            collective_id=0, has_side_effects=True, vmem_limit_bytes=62 * 2**20
        ),
    )(
        coeffs,
        columns.reshape(1, STICKS),
        potential,
        ritz_vectors,
        jnp.asarray(inverse),
        jnp.asarray(forward),
        jnp.asarray(wave_table()),
    )
    anywhere = pl.BlockSpec(memory_space=pl.ANY)
    refined, refined_h, values = pl.pallas_call(
        emit,
        out_shape=outs,
        in_specs=[vmem] * 3,
        out_specs=(vmem,) * 3,
        compiler_params=pltpu.CompilerParams(vmem_limit_bytes=2**20),
    )(*results)
    return refined, refined_h, values.reshape(BANDS)


def solution(mesh):
    return jax.shard_map(
        shards,
        mesh=mesh,
        in_specs=(P("band", "pencil", None), P(), P("pencil", None), P()),
        out_specs=(P("band", "pencil", None), P("band", "pencil", None), P()),
        check_vma=False,
    )
```
